256 devices in a mesh: fibre: 8 (over y, core), record: 32 (over x, z).
Axes of the slice: x: 4, y: 4, z: 8, core: 2. Of those that a mesh axis runs over, the one named last changes fastest.
Arguments:
- records: bfloat16 [32, 64, 64, 1024], P('record', 'fibre'), may hold values from -80 to 80, as said below
- labels: int32 [32, 64, 1024], P('record', 'fibre'), may hold values from 0 to 1
- w_time: bfloat16 [7, 64, 64], replicated, may hold values from -0.25 to 0.25
- b_time: float32 [64], replicated, may hold values from -3 to 3
- w_fibre: bfloat16 [7, 64, 64], replicated, may hold values from -0.25 to 0.25
- gamma: float32 [64], replicated, may hold values from 0.1 to 1.9
- beta: float32 [64], replicated, may hold values from -3 to 3
- w_head: bfloat16 [64], replicated, may hold values from -0.75 to 0.75
- b_head: float32 [1], replicated, may hold values from -3 to 3
Outputs:
- grad_records: bfloat16 [32, 64, 64, 1024], P('record', 'fibre')
- grad_w_time: float32 [7, 64, 64], replicated
- grad_b_time: float32 [64], replicated
- grad_w_fibre: float32 [7, 64, 64], replicated
- grad_gamma: float32 [64], replicated
- grad_beta: float32 [64], replicated
- grad_w_head: float32 [64], replicated
- loss: float32 [], replicated
The draws below stay inside these ranges and needn't reach their ends.
Inputs may be any that keep to these rules, and one draw needn't show every extreme that they name: `records`: field samples.
All inputs are finite; a program needn't handle non-finite values.
Results may differ from the reference program's by a relative error of at most 0.0081.
Values may be sent and summed in bfloat16 or wider, within the bound.
A program may use at most 64 MiB of HBM per device.

```python
import jax
import jax.numpy as jnp
from jax import lax

F = 64
TEMPORAL_TAPS = 7
TIME_DILATION = 2
KC = 7
SAMPLES = 1024
RECORDS = 32
CHANNELS = 64


def draw_records(key, part):
    key = jax.random.fold_in(key, 17)
    first_key, second_key = jax.random.split(key, 2)
    shape = (RECORDS, CHANNELS, F, SAMPLES)
    order = jnp.arange(RECORDS, dtype=jnp.float32) / max(RECORDS - 1, 1)
    along = jnp.arange(CHANNELS, dtype=jnp.float32) / max(CHANNELS - 1, 1)
    when = jnp.arange(SAMPLES, dtype=jnp.float32) / max(SAMPLES - 1, 1)
    base = jnp.clip(jax.random.normal(first_key, shape, jnp.float32), -4.0, 4.0)
    rise = 1.0 + 2.0 * order
    channel_rise = 1.0 + 2.0 * along
    envelope = 0.2 * jnp.exp(jnp.log(5.0) * when)
    rough = jnp.exp(jax.random.uniform(second_key, (RECORDS, CHANNELS, 1, 1), jnp.float32, -0.35, 0.35))
    return (base * rise[:, None, None, None] * channel_rise[None, :, None, None] * envelope[None, None, None, :] * rough).astype(jnp.bfloat16)


def draw_labels(key, part):
    key = jax.random.fold_in(key, 23)
    picks = jax.random.randint(key, (RECORDS, CHANNELS, SAMPLES), 0, 20, dtype=jnp.int32)
    sample_index = jnp.arange(SAMPLES, dtype=jnp.int32)
    threshold = 1 + 9 * sample_index // SAMPLES
    return (picks < threshold[None, None, :]).astype(jnp.int32)


def centred(key, shape, deviation, reach, kind=jnp.bfloat16):
    drawn = deviation * jax.random.normal(key, shape, jnp.float32)
    return jnp.clip(drawn, min=-reach, max=reach).astype(kind)


def setup_inputs(seed: int = 0) -> dict:
    seeds = jax.random.split(jax.random.key(seed), 10)
    records = draw_records(jax.random.fold_in(seeds[9], 71), 0)
    labels = draw_labels(jax.random.fold_in(seeds[9], 71), 0)
    w_time = centred(seeds[2], (TEMPORAL_TAPS, F, F), (TEMPORAL_TAPS * F) ** -0.5, 0.25)
    b_time = centred(seeds[3], (F,), 0.5, 3.0, jnp.float32)
    w_fibre = centred(seeds[4], (KC, F, F), (KC * F) ** -0.5, 0.25)
    gamma = jnp.clip(1.0 + 0.18 * jax.random.normal(seeds[5], (F,), jnp.float32), 0.1, 1.9)
    beta = centred(seeds[6], (F,), 0.5, 3.0, jnp.float32)
    w_head = centred(seeds[7], (F,), F ** -0.5, 0.75)
    b_head = centred(seeds[8], (1,), 1.0, 3.0, jnp.float32)
    return dict(records=records, labels=labels, w_time=w_time, b_time=b_time, w_fibre=w_fibre, gamma=gamma, beta=beta, w_head=w_head, b_head=b_head)


EPS = 1e-05

def silu_slope(value):
    sig = jax.nn.sigmoid(value)
    return sig * (1.0 + value * (1.0 - sig))

def time_conv(strain_field, weights):
    window_size = strain_field.shape[2]
    halfwidth = (weights.shape[0] - 1) // 2
    padded_input = jnp.pad(strain_field.astype(jnp.float32), ((0, 0), (0, 0), (TIME_DILATION * halfwidth, TIME_DILATION * halfwidth)))
    complete_weight = weights.astype(jnp.float32)
    grand_total = jnp.zeros((strain_field.shape[0], weights.shape[1], window_size), jnp.float32)
    for tap_index in range(weights.shape[0]):
        grand_total = grand_total + jnp.einsum('mz,kzv->kmv', complete_weight[tap_index], padded_input[:, :, TIME_DILATION * tap_index:TIME_DILATION * tap_index + window_size])
    return grand_total

def fibre_conv(strain_field, weights):
    count = strain_field.shape[0]
    halfwidth = (weights.shape[0] - 1) // 2
    padded_input = jnp.pad(strain_field.astype(jnp.float32), ((halfwidth, halfwidth), (0, 0), (0, 0)))
    complete_weight = weights.astype(jnp.float32)
    grand_total = jnp.zeros((count, weights.shape[1], strain_field.shape[2]), jnp.float32)
    for tap_index in range(weights.shape[0]):
        grand_total = grand_total + jnp.einsum('mz,kzv->kmv', complete_weight[tap_index], padded_input[tap_index:tap_index + count])
    return grand_total

def reference(records, labels, w_time, b_time, w_fibre, gamma, beta, w_head, b_head):
    cell_count_total = jnp.float32(RECORDS * CHANNELS * SAMPLES)
    cells = jnp.float32(CHANNELS * SAMPLES)
    temporal_halfwidth = (TEMPORAL_TAPS - 1) // 2
    half_c = (KC - 1) // 2

    def forward(strain_field):
        pre = time_conv(strain_field, w_time) + b_time[None, :, None]
        hidden = jax.nn.silu(pre).astype(jnp.bfloat16)
        return (hidden, fibre_conv(hidden, w_fibre))
    hidden_all, z2_all = lax.map(forward, records)
    channel_mean = lax.optimization_barrier(jnp.sum(lax.map(lambda z: lax.optimization_barrier(jnp.sum(z, axis=(0, 2))), z2_all), axis=0)) / cell_count_total
    spread = lax.map(lambda z: lax.optimization_barrier(jnp.sum((z - channel_mean[None, :, None]) ** 2, axis=(0, 2))), z2_all)
    var = lax.optimization_barrier(jnp.sum(spread, axis=0)) / cell_count_total
    inverse_deviation = lax.rsqrt(var + EPS)
    head_w = w_head.astype(jnp.float32)

    def head_output(second_preactivation, phase_label):
        normalized_input = (second_preactivation - channel_mean[None, :, None]) * inverse_deviation[None, :, None]
        activation = gamma[None, :, None] * normalized_input + beta[None, :, None]
        h2 = jax.nn.silu(activation).astype(jnp.bfloat16)
        logit = jnp.einsum('cfs,f->cs', h2.astype(jnp.float32), head_w) + b_head[0]
        target = phase_label.astype(jnp.float32)
        partial_loss = jnp.sum(jnp.log1p(jnp.exp(logit)) - target * logit)
        dlogit = jax.nn.sigmoid(logit) - target
        head_output_gradient = jnp.einsum('cs,cfs->f', dlogit, h2.astype(jnp.float32))
        dh2 = (dlogit[:, None, :] * head_w[None, :, None]).astype(jnp.bfloat16)
        activation_gradient = dh2.astype(jnp.float32) * silu_slope(activation)
        return (normalized_input, partial_loss, head_output_gradient, activation_gradient)

    def first_pass(items):
        second_preactivation, phase_label = items
        normalized_input, partial_loss, head_output_gradient, activation_gradient = head_output(second_preactivation, phase_label)
        return (partial_loss, head_output_gradient, lax.optimization_barrier(jnp.sum(activation_gradient, axis=(0, 2))), lax.optimization_barrier(jnp.sum(activation_gradient * normalized_input, axis=(0, 2))))
    loss_parts, head_parts, beta_parts, gamma_parts = lax.map(first_pass, (z2_all, labels))
    beta_total_sum = lax.optimization_barrier(jnp.sum(beta_parts, axis=0))
    gamma_total_sum = lax.optimization_barrier(jnp.sum(gamma_parts, axis=0))
    wt = w_time.astype(jnp.float32)
    wf = w_fibre.astype(jnp.float32)

    def second_pass(items):
        strain_field, hidden, second_preactivation, phase_label = items
        normalized_input, partial_loss, head_output_gradient, activation_gradient = head_output(second_preactivation, phase_label)
        second_preact_gradient = (gamma[None, :, None] * inverse_deviation[None, :, None] * (activation_gradient - beta_total_sum[None, :, None] / cell_count_total - normalized_input * gamma_total_sum[None, :, None] / cell_count_total)).astype(jnp.bfloat16)
        dz2f = second_preact_gradient.astype(jnp.float32)
        count = hidden.shape[0]
        hidden_pad = jnp.pad(hidden.astype(jnp.float32), ((half_c, half_c), (0, 0), (0, 0)))
        dz2_pad = jnp.pad(dz2f, ((half_c, half_c), (0, 0), (0, 0)))
        fibre_grad = jnp.stack([jnp.einsum('uqp,ubp->qb', dz2f, hidden_pad[tap_index:tap_index + count]) for tap_index in range(KC)])
        dh1 = jnp.zeros(hidden.shape, jnp.float32)
        for tap_index in range(KC):
            dh1 = dh1 + jnp.einsum('gf,cgs->cfs', wf[tap_index], dz2_pad[2 * half_c - tap_index:2 * half_c - tap_index + count])
        dh1 = dh1.astype(jnp.bfloat16)
        pre = time_conv(strain_field, w_time) + b_time[None, :, None]
        dz1 = (dh1.astype(jnp.float32) * silu_slope(pre)).astype(jnp.bfloat16)
        first_preact_gradient_flat = dz1.astype(jnp.float32)
        bias_grad = lax.optimization_barrier(jnp.sum(first_preact_gradient_flat, axis=(0, 2)))
        window_size = strain_field.shape[2]
        padding_amount = TIME_DILATION * temporal_halfwidth
        strain_field_padded = jnp.pad(strain_field.astype(jnp.float32), ((0, 0), (0, 0), (padding_amount, padding_amount)))
        dz1_pad = jnp.pad(first_preact_gradient_flat, ((0, 0), (0, 0), (padding_amount, padding_amount)))
        temporal_gradient = jnp.stack([jnp.einsum('uqp,ubp->qb', first_preact_gradient_flat, strain_field_padded[:, :, TIME_DILATION * tap_index:TIME_DILATION * tap_index + window_size]) for tap_index in range(TEMPORAL_TAPS)])
        back = jnp.zeros(strain_field.shape, jnp.float32)
        for tap_index in range(TEMPORAL_TAPS):
            window_start = TIME_DILATION * (2 * temporal_halfwidth - tap_index)
            back = back + jnp.einsum('gf,cgs->cfs', wt[tap_index], dz1_pad[:, :, window_start:window_start + window_size])
        return (back.astype(jnp.bfloat16), temporal_gradient, bias_grad, fibre_grad)
    grad_records, time_parts, bias_parts, fibre_parts = lax.map(second_pass, (records, hidden_all, z2_all, labels))
    grad_w_time = lax.optimization_barrier(jnp.sum(time_parts, axis=0)) / cells
    grad_b_time = lax.optimization_barrier(jnp.sum(bias_parts, axis=0)) / cells
    grad_w_fibre = lax.optimization_barrier(jnp.sum(fibre_parts, axis=0)) / cells
    grad_gamma = gamma_total_sum / cells
    grad_beta = beta_total_sum / cells
    grad_w_head = lax.optimization_barrier(jnp.sum(head_parts, axis=0)) / cells
    loss = jnp.sum(loss_parts) / cell_count_total
    return (grad_records, grad_w_time, grad_b_time, grad_w_fibre, grad_gamma, grad_beta, grad_w_head, loss)
```

```python
import functools

import jax
import jax.numpy as jnp
from jax import lax
from jax.experimental import pallas as pl
from jax.experimental.pallas import tpu as pltpu
from jax.sharding import PartitionSpec as P

F = 64
TAPS = 7
DILATION = 2
HALF = 3
EPS = 1e-05
BF = jnp.bfloat16
F32 = jnp.float32
MESH = pl.DeviceIdType.MESH
NT = (((1,), (1,)), ((), ()))


def mm(a, b):
    return jnp.dot(a, b, preferred_element_type=F32)


def sigmoid(v):
    return 1.0 / (1.0 + jnp.exp(-v))


def eye():
    return lax.broadcasted_iota(jnp.int32, (F, F), 0) == lax.broadcasted_iota(jnp.int32, (F, F), 1)


def to_col(row):
    return jnp.sum(jnp.where(eye(), jnp.broadcast_to(row, (F, F)), 0.0), axis=1, keepdims=True)


def to_row(col):
    return jnp.sum(jnp.where(eye(), jnp.broadcast_to(col, (F, F)), 0.0), axis=0, keepdims=True)


def wide(row):
    return jnp.broadcast_to(to_col(row), (F, 128))


class Group:
    def __init__(self, n, me, target, send, recv):
        self.n, self.me, self.target, self.send, self.recv = n, me, target, send, recv

    def peers(self):
        return [lax.rem(self.me + d, self.n) for d in range(1, self.n)]

    def copy(self, src, dst, p, slot):
        return pltpu.make_async_remote_copy(
            src_ref=src,
            dst_ref=dst,
            send_sem=self.send.at[p],
            recv_sem=self.recv.at[slot],
            device_id=self.target(p),
            device_id_type=MESH,
        )

    def spread(self, buf):
        for p in self.peers():
            self.copy(buf.at[self.me], buf.at[self.me], p, self.me).start()

    def scatter(self, src, buf):
        for p in self.peers():
            self.copy(src.at[p], buf.at[self.me], p, self.me).start()

    def arrive(self, buf):
        for p in self.peers():
            self.copy(buf.at[p], buf.at[p], p, p).wait_recv()

    def done(self, buf):
        for p in self.peers():
            self.copy(buf.at[p], buf.at[p], p, p).wait_send()


def kernel(
    dims,
    x_ref, lab_ref, wt_ref, bt_ref, wf_ref, gam_ref, bet_ref, wh_ref, bh_ref,
    gr_ref, gwt_ref, gbt_ref, gwf_ref, gga_ref, gbe_ref, gwh_ref, loss_ref,
    wts, wtt, wfb, wfr, xcol, dcol, h1, sl1, z2, sl2, dz2, dz1, par, acc, accr, lab, dl, dll, dlr,
    gt,
    sf1, sx1, sz1, sf2, sx2, sz2,
    ga, ra, xa, za, fa, gb, rb, xb, zb, fb,
    hs, hr, ds, dr,
    f1s, f1r, x1s, x1r, z1s, z1r, f2s, f2r, x2s, x2r, z2s, z2r,
    a1s, a1r, a2s, a2r, a3s, a3r, a4s, a4r,
    b1s, b1r, b2s, b2r, b3s, b3r, b4s, b4r,
):
    nf, nx, nz, C, T = dims
    total = float(nf * nx * nz * C * T)
    cells = float(nf * C * T)
    fi = lax.axis_index("fibre")
    ri = lax.axis_index("record")
    xi, zi = ri // nz, lax.rem(ri, nz)

    def to_f(p):
        return (p, ri)

    def to_x(p):
        return (fi, p * nz + zi)

    def to_z(p):
        return (fi, xi * nz + p)

    def group_f(s, r):
        return Group(nf, fi, to_f, s, r)

    def group_x(s, r):
        return Group(nx, xi, to_x, s, r)

    def group_z(s, r):
        return Group(nz, zi, to_z, s, r)

    barrier = pltpu.get_barrier_semaphore()
    for group in (group_f(None, None), group_x(None, None), group_z(None, None)):
        for p in group.peers():
            pl.semaphore_signal(barrier, inc=1, device_id=group.target(p), device_id_type=MESH)

    for k in range(TAPS):
        wts[:, k * F:(k + 1) * F] = wt_ref[k]
        wtt[:, k * F:(k + 1) * F] = wt_ref[k].astype(F32).T.astype(BF)
    wfb[...] = jnp.zeros_like(wfb)
    wfr[...] = jnp.zeros_like(wfr)
    for k in range(TAPS):
        w = wf_ref[k]
        wr = wf_ref[TAPS - 1 - k].astype(F32).T.astype(BF)
        for j in range(4):
            wfb[j * F:(j + 1) * F, (j + k) * F:(j + k + 1) * F] = w
            wfr[j * F:(j + 1) * F, (j + k) * F:(j + k + 1) * F] = wr
    for c in range(C):
        lab[c] = lab_ref[c:c + 1, :].astype(F32)
    par[0] = wide(bt_ref[...])
    acc[...] = jnp.zeros_like(acc)
    accr[...] = jnp.zeros_like(accr)

    pl.semaphore_wait(barrier, nf + nx + nz - 3)

    has_l, has_r = fi > 0, fi < nf - 1
    left, right = lax.rem(fi + nf - 1, nf), lax.rem(fi + 1, nf)

    @pl.when(jnp.logical_not(has_l))
    def _():
        for i in range(2 * HALF):
            h1[i] = jnp.zeros((F, T), BF)
        for i in range(HALF):
            dz2[i] = jnp.zeros((F, T), BF)

    @pl.when(jnp.logical_not(has_r))
    def _():
        for i in range(2 * HALF):
            h1[2 * HALF + C + i] = jnp.zeros((F, T), BF)
        for i in range(HALF):
            dz2[HALF + C + i] = jnp.zeros((F, T), BF)

    def halo(c, side):
        slot = c + 2 * HALF + C if side == "l" else c + 2 * HALF - C
        index = c + 2 * HALF if side == "l" else c + 2 * HALF - C
        return pltpu.make_async_remote_copy(
            src_ref=h1.at[c + 2 * HALF],
            dst_ref=h1.at[slot],
            send_sem=hs.at[index],
            recv_sem=hr.at[index],
            device_id=(left if side == "l" else right, ri),
            device_id_type=MESH,
        )

    def halo_arrive(i, side):
        slot = i if side == "l" else i + 2 * HALF + C
        index = i if side == "l" else i + 2 * HALF
        pltpu.make_async_remote_copy(
            src_ref=h1.at[slot], dst_ref=h1.at[slot], send_sem=hs.at[index], recv_sem=hr.at[index],
            device_id=(left if side == "l" else right, ri), device_id_type=MESH,
        ).wait_recv()

    lane = lax.broadcasted_iota(jnp.int32, (F, 128), 1)

    def shifted(src, dst, sign):
        for k in range(TAPS):
            s = sign * DILATION * (k - HALF)
            rows = slice(k * F, (k + 1) * F)
            if s == 0:
                dst[rows, :] = src.astype(BF)
                continue
            r = pltpu.roll(src, (-s) % T, 1)
            dst[rows, :] = r.astype(BF)
            if s > 0:
                dst[rows, T - 128:] = jnp.where(lane < 128 - s, r[:, T - 128:], 0.0).astype(BF)
            else:
                dst[rows, :128] = jnp.where(lane >= -s, r[:, :128], 0.0).astype(BF)

    def forward(i, carry):
        c = jnp.where(lax.rem(i, 2) == 0, i // 2, C - 1 - i // 2)
        shifted(x_ref[c].astype(F32), xcol.at[c], 1)
        for n in range(0, T, 256):
            pre2 = mm(wts[...], xcol[c, :, n:n + 256])
            for m in range(0, 256, 128):
                cols = slice(n + m, n + m + 128)
                pre = pre2[:, m:m + 128] + par[0]
                s = sigmoid(pre)
                h = pre * s
                h1[c + 2 * HALF, :, cols] = h.astype(BF)
                sl1[c, :, cols] = s + h * (1.0 - s)

        @pl.when(jnp.logical_and(has_l, c < HALF))
        def _():
            halo(c, "l").start()

        @pl.when(jnp.logical_and(has_r, c >= C - HALF))
        def _():
            halo(c, "r").start()

        return carry

    lax.fori_loop(0, C, forward, 0)
    for d in range(HALF):
        @pl.when(has_l)
        def _():
            halo(HALF + d, "l").start()

        @pl.when(has_r)
        def _():
            halo(C - HALF - 1 - d, "r").start()

    def fibre_conv(first, count, lo):
        def body(n, carry):
            cols = pl.ds(pl.multiple_of(n * 256, 256), 256)
            data = h1[lo:lo + count + 2 * HALF, :, cols].reshape((count + 2 * HALF) * F, 256)
            out = mm(wfb[:count * F, :(count + 2 * HALF) * F], data)
            z2[first:first + count, :, cols] = out.reshape(count, F, 256)
            return carry

        lax.fori_loop(0, T // 256, body, 0)

    @pl.when(has_l)
    def _():
        for i in range(HALF):
            halo_arrive(HALF + i, "l")

    fibre_conv(HALF, 4, HALF)

    @pl.when(has_r)
    def _():
        for i in range(HALF):
            halo_arrive(i, "r")

    fibre_conv(HALF + 4, 4, HALF + 4)

    def add_up(c, total_):
        for n in range(0, T, 128):
            total_ = total_ + z2[HALF + c, :, n:n + 128]
        return total_

    zero = jnp.zeros((F, 128), F32)
    own_mean = jnp.sum(lax.fori_loop(0, C, add_up, zero), axis=1, keepdims=True) / float(C * T)
    own_wide = jnp.broadcast_to(own_mean, (F, 128))

    def spread_up(c, total_):
        for n in range(0, T, 128):
            d = z2[HALF + c, :, n:n + 128] - own_wide
            total_ = total_ + d * d
        return total_

    own_m2 = jnp.sum(lax.fori_loop(0, C, spread_up, zero), axis=1, keepdims=True)
    sub = lax.broadcasted_iota(jnp.int32, (8, 128), 0)

    def tile(row0, row1):
        r0 = jnp.concatenate([row0, row0], axis=1)
        r1 = jnp.concatenate([row1, row1], axis=1)
        return jnp.where(sub == 0, jnp.broadcast_to(r0, (8, 128)), jnp.where(sub == 1, jnp.broadcast_to(r1, (8, 128)), 0.0))

    def merge(buf, n, count):
        value = [buf[i] for i in range(n)]
        avg = functools.reduce(jnp.add, value) * (1.0 / n)
        m2 = functools.reduce(jnp.add, [(v - avg) * (v - avg) for v in value]) * count
        return jnp.where(sub == 1, avg * n + pltpu.roll(m2, 1, 0), avg)

    def plain(buf, n):
        return functools.reduce(jnp.add, [buf[i] for i in range(n)])

    g_f1, g_x1, g_z1 = group_f(f1s, f1r), group_x(x1s, x1r), group_z(z1s, z1r)
    sf1[fi] = tile(to_row(own_mean), to_row(own_m2))
    g_f1.spread(sf1)
    g_f1.arrive(sf1)
    sx1[xi] = merge(sf1, nf, float(C * T))
    g_x1.spread(sx1)

    @pl.when(has_l)
    def _():
        for i in range(HALF):
            halo_arrive(i, "l")
        fibre_conv(0, HALF, 0)

    g_x1.arrive(sx1)
    sz1[zi] = merge(sx1, nx, float(C * T * nf))
    g_z1.spread(sz1)

    @pl.when(has_r)
    def _():
        for i in range(HALF):
            halo_arrive(HALF + i, "r")
        fibre_conv(HALF + C, HALF, HALF + C)

    g_z1.arrive(sz1)
    stats = merge(sz1, nz, float(C * T * nf * nx))
    mean_row = stats[0:1, :F]
    rstd_row = lax.rsqrt(stats[1:2, :F] / total + EPS)
    par[1] = wide(mean_row)
    par[2] = wide(gam_ref[...] * rstd_row)
    par[3] = wide(bet_ref[...])
    par[4] = wide(wh_ref[...].astype(F32))
    par[5] = wide(rstd_row)

    bias = bh_ref[0, 0]

    def head(c, carry):
        for n in range(0, T, 128):
            cols = slice(n, n + 128)
            zc = z2[HALF + c, :, cols] - par[1]
            act = zc * par[2] + par[3]
            s = sigmoid(act)
            h = act * s
            h2 = h.astype(BF).astype(F32)
            logit = jnp.sum(h2 * par[4], axis=0, keepdims=True) + bias
            target = lab[c, :, cols]
            soft = jnp.maximum(logit, 0.0) + jnp.log1p(jnp.exp(-jnp.abs(logit)))
            accr[0:1, :] += soft - target * logit
            dlogit = sigmoid(logit) - target
            dl[c, :, cols] = dlogit
            dh2 = (dlogit * par[4]).astype(BF).astype(F32)
            dact = dh2 * (s + h * (1.0 - s))
            sl2[HALF + c, :, cols] = dact
            acc[0] += dact
            acc[1] += dact * zc
            acc[2] += dlogit * h2
        return carry

    lax.fori_loop(0, C, head, 0)

    def dl_copy(side):
        i = 0 if side == "l" else 1
        return pltpu.make_async_remote_copy(
            src_ref=dl.at[0:HALF] if side == "l" else dl.at[C - HALF:C], dst_ref=dlr if side == "l" else dll, send_sem=ds.at[i], recv_sem=dr.at[i],
            device_id=(left if side == "l" else right, ri), device_id_type=MESH,
        )

    def dl_arrive(side):
        i = 1 if side == "l" else 0
        buf = dll if side == "l" else dlr
        pltpu.make_async_remote_copy(
            src_ref=buf, dst_ref=buf, send_sem=ds.at[i], recv_sem=dr.at[i],
            device_id=(left if side == "l" else right, ri), device_id_type=MESH,
        ).wait_recv()

    @pl.when(has_l)
    def _():
        dl_copy("l").start()

    @pl.when(has_r)
    def _():
        dl_copy("r").start()

    def lanes(v):
        return jnp.sum(v, axis=1, keepdims=True)

    g_f2, g_x2, g_z2 = group_f(f2s, f2r), group_x(x2s, x2r), group_z(z2s, z2r)
    sf2[fi] = tile(to_row(lanes(acc[0])), to_row(lanes(acc[1])))
    g_f2.spread(sf2)

    def halo_dact(slot, buf, row):
        for n in range(0, T, 128):
            cols = slice(n, n + 128)
            act = (z2[slot, :, cols] - par[1]) * par[2] + par[3]
            s = sigmoid(act)
            dh2 = (buf[row, :, cols] * par[4]).astype(BF).astype(F32)
            sl2[slot, :, cols] = dh2 * (s + act * s * (1.0 - s))

    def halo_left(i, carry):
        halo_dact(i, dll, i)
        return carry

    def halo_right(i, carry):
        halo_dact(HALF + C + i, dlr, i)
        return carry

    g_f2.arrive(sf2)
    sx2[xi] = plain(sf2, nf)
    g_x2.spread(sx2)

    @pl.when(has_l)
    def _():
        dl_arrive("l")
        lax.fori_loop(0, HALF, halo_left, 0)

    g_x2.arrive(sx2)
    sz2[zi] = plain(sx2, nx)
    g_z2.spread(sz2)

    @pl.when(has_r)
    def _():
        dl_arrive("r")
        lax.fori_loop(0, HALF, halo_right, 0)

    g_z2.arrive(sz2)
    sums = plain(sz2, nz)
    rstd_row = to_row(par[5][:, 0:1])
    beta_row = sums[0:1, :F]
    gamma_row = sums[1:2, :F] * rstd_row
    gbe_ref[...] = beta_row / cells
    gga_ref[...] = gamma_row / cells
    par[6] = wide(beta_row / total)
    par[7] = wide(gamma_row * rstd_row / total)

    def slope_back(slot, carry):
        for n in range(0, T, 128):
            cols = slice(n, n + 128)
            zc = z2[slot, :, cols] - par[1]
            dz2[slot, :, cols] = (par[2] * (sl2[slot, :, cols] - par[6] - zc * par[7])).astype(BF)
        return carry

    lax.fori_loop(jnp.where(has_l, 0, HALF), jnp.where(has_r, C + 2 * HALF, C + HALF), slope_back, 0)

    for q in range(2):
        grad = lax.dot_general(
            dz2[HALF + 4 * q:HALF + 4 * q + 4].reshape(4 * F, T),
            h1[HALF + 4 * q:HALF + 4 * q + 10].reshape(10 * F, T),
            NT, preferred_element_type=F32,
        )
        for j in range(4):
            piece = grad[j * F:(j + 1) * F, j * F:(j + TAPS) * F]
            if q == 0 and j == 0:
                gt[:, :TAPS * F] = piece
            else:
                gt[:, :TAPS * F] += piece
    col = lax.broadcasted_iota(jnp.int32, (F, F), 1)

    def pack(src, dst, first, second):
        src[:, TAPS * F:] = jnp.where(col == 0, jnp.broadcast_to(first, (F, F)), jnp.where(col == 1, jnp.broadcast_to(second, (F, F)), 0.0))
        for i in range(nf):
            rows = F // nf
            dst[i] = src[i * rows:(i + 1) * rows, :]

    loss_part = jnp.sum(accr[0:1, :], axis=1, keepdims=True)
    pack(gt, ga, lanes(acc[2]), jnp.where(lax.broadcasted_iota(jnp.int32, (F, 1), 0) == 0, jnp.broadcast_to(loss_part, (F, 1)), 0.0))
    a1, a2, a3, a4 = group_f(a1s, a1r), group_x(a2s, a2r), group_z(a3s, a3r), group_f(a4s, a4r)
    b1, b2, b3, b4 = group_f(b1s, b1r), group_x(b2s, b2r), group_z(b3s, b3r), group_f(b4s, b4r)
    a1.scatter(ga, ra)
    ra[fi] = ga[fi]

    def fibre_back(q):
        def body(n, carry):
            cols = pl.ds(pl.multiple_of(n * 256, 256), 256)
            data = dz2[4 * q:4 * q + 10, :, cols].reshape(10 * F, 256)
            out = mm(wfr[...], data).reshape(4, F, 256)
            for j in range(4):
                dh = out[j].astype(BF).astype(F32)
                value = (dh * sl1[4 * q + j, :, cols]).astype(BF)
                dz1[4 * q + j, :, cols] = value
                value = value.astype(F32)
                acc[3] += value[:, :128] + value[:, 128:]
            return carry

        lax.fori_loop(0, T // 256, body, 0)

    fibre_back(0)
    a1.arrive(ra)
    xa[xi] = plain(ra, nf)
    a2.spread(xa)
    fibre_back(1)
    a2.arrive(xa)
    za[zi] = plain(xa, nx)
    a3.spread(za)

    gt[...] = jnp.zeros_like(gt)

    def time_grad(c, carry):
        gt[:, :TAPS * F] += lax.dot_general(dz1[c], xcol[c], NT, preferred_element_type=F32)
        return carry

    lax.fori_loop(0, C, time_grad, 0)
    a3.arrive(za)
    fa[fi] = plain(za, nz)
    pack(gt, gb, lanes(acc[3]), jnp.zeros((F, 1), F32))
    b1.scatter(gb, rb)
    rb[fi] = gb[fi]
    a4.spread(fa)

    def time_back(c, carry):
        shifted(dz1[c].astype(F32), dcol, -1)
        for n in range(0, T, 256):
            gr_ref[c, :, n:n + 256] = mm(wtt[...], dcol[:, n:n + 256]).astype(BF)
        return carry

    lax.fori_loop(0, 2, time_back, 0)
    b1.arrive(rb)
    xb[xi] = plain(rb, nf)
    b2.spread(xb)
    lax.fori_loop(2, 4, time_back, 0)
    b2.arrive(xb)
    zb[zi] = plain(xb, nx)
    b3.spread(zb)
    lax.fori_loop(4, 6, time_back, 0)
    b3.arrive(zb)
    fb[fi] = plain(zb, nz)
    b4.spread(fb)
    lax.fori_loop(6, C, time_back, 0)

    a4.arrive(fa)
    rows = F // nf
    for i in range(nf):
        value = fa[i] / cells
        for k in range(TAPS):
            gwf_ref[k, i * rows:(i + 1) * rows, :] = value[:, k * F:(k + 1) * F]
    tail = fa[...].reshape(F, 8 * F)[:, TAPS * F:]
    gwh_ref[...] = to_row(tail[:, 0:1] / cells)
    loss_ref[...] = tail[0:1, 1:2] / total
    b4.arrive(fb)
    for i in range(nf):
        value = fb[i] / cells
        for k in range(TAPS):
            gwt_ref[k, i * rows:(i + 1) * rows, :] = value[:, k * F:(k + 1) * F]
    tail = fb[...].reshape(F, 8 * F)[:, TAPS * F:]
    gbt_ref[...] = to_row(tail[:, 0:1] / cells)

    for group, buf in (
        (g_f1, sf1), (g_x1, sx1), (g_z1, sz1), (g_f2, sf2), (g_x2, sx2), (g_z2, sz2),
        (a1, ga), (a2, xa), (a3, za), (a4, fa), (b1, gb), (b2, xb), (b3, zb), (b4, fb),
    ):
        group.done(buf)

    @pl.when(has_l)
    def _():
        dl_copy("l").wait_send()
        for c in range(2 * HALF):
            halo(c, "l").wait_send()

    @pl.when(has_r)
    def _():
        dl_copy("r").wait_send()
        for c in range(2 * HALF):
            halo(C - 1 - c, "r").wait_send()


def local(dims, records, labels, w_time, b_time, w_fibre, gamma, beta, w_head, b_head):
    nf, nx, nz, C, T = dims
    vm = pl.BlockSpec(memory_space=pltpu.VMEM)
    S = jax.ShapeDtypeStruct
    V = pltpu.VMEM
    D = pltpu.SemaphoreType.DMA
    rows = F // nf

    def small():
        return [V((nf, 8, 128), F32), V((nx, 8, 128), F32), V((nz, 8, 128), F32)]

    def large():
        return [V((nf, rows, 512), F32), V((nf, rows, 512), F32), V((nx, rows, 512), F32),
                V((nz, rows, 512), F32), V((nf, rows, 512), F32)]

    def sems(*sizes):
        return [D((n,)) for n in sizes for _ in range(2)]

    outs = pl.pallas_call(
        functools.partial(kernel, dims),
        out_shape=(
            S((C, F, T), BF), S((TAPS, F, F), F32), S((1, F), F32), S((TAPS, F, F), F32),
            S((1, F), F32), S((1, F), F32), S((1, F), F32), S((1, 1), F32),
        ),
        in_specs=[vm] * 8 + [pl.BlockSpec(memory_space=pltpu.SMEM)],
        out_specs=[vm] * 8,
        scratch_shapes=[
            V((F, TAPS * F), BF), V((F, TAPS * F), BF), V((4 * F, 10 * F), BF), V((4 * F, 10 * F), BF),
            V((C, TAPS * F, T), BF), V((TAPS * F, T), BF), V((C + 12, F, T), BF), V((C, F, T), F32),
            V((C + 6, F, T), F32), V((C + 6, F, T), F32), V((C + 6, F, T), BF), V((C, F, T), BF),
            V((8, F, 128), F32), V((4, F, 128), F32), V((8, 128), F32),
            V((C, 1, T), F32), V((C, 1, T), F32), V((HALF, 1, T), F32), V((HALF, 1, T), F32), V((F, 512), F32),
            *small(), *small(), *large(), *large(),
            *sems(12, 2), *sems(nf, nx, nz), *sems(nf, nx, nz),
            *sems(nf, nx, nz, nf), *sems(nf, nx, nz, nf),
        ],
        compiler_params=pltpu.CompilerParams(
            collective_id=0, has_side_effects=True, vmem_limit_bytes=56 * 1024 * 1024
        ),
    )(
        records[0], labels[0], w_time, b_time.reshape(1, F), w_fibre, gamma.reshape(1, F), beta.reshape(1, F),
        w_head.reshape(1, F), b_head.reshape(1, 1),
    )
    gr, gwt, gbt, gwf, gga, gbe, gwh, loss = outs
    return gr[None], gwt, gbt[0], gwf, gga[0], gbe[0], gwh[0], loss[0, 0]


def solution(mesh):
    nf, nr = mesh.shape["fibre"], mesh.shape["record"]
    nx = 4 if nr % 4 == 0 else 1

    def run(records, *rest):
        dims = (nf, nx, nr // nx, records.shape[1] // nf, records.shape[3])
        return jax.shard_map(
            functools.partial(local, dims),
            mesh=mesh,
            in_specs=(P("record", "fibre", None, None), P("record", "fibre", None)) + (P(),) * 7,
            out_specs=(P("record", "fibre", None, None),) + (P(),) * 7,
            check_vma=False,
        )(records, *rest)

    return run
```

```python
import functools

import jax
import jax.numpy as jnp
from jax import lax
from jax.experimental import pallas as pl
from jax.experimental.pallas import tpu as pltpu
from jax.sharding import PartitionSpec as P

F = 64
TAPS = 7
DILATION = 2
HALF = 3
EPS = 1e-05
BF = jnp.bfloat16
F32 = jnp.float32
MESH = pl.DeviceIdType.MESH
NT = (((1,), (1,)), ((), ()))


def mm(a, b):
    return jnp.dot(a, b, preferred_element_type=F32)


def sigmoid(v):
    return 0.5 * jnp.tanh(0.5 * v) + 0.5


def eye():
    return lax.broadcasted_iota(jnp.int32, (F, F), 0) == lax.broadcasted_iota(jnp.int32, (F, F), 1)


def to_col(row):
    return jnp.sum(jnp.where(eye(), jnp.broadcast_to(row, (F, F)), 0.0), axis=1, keepdims=True)


def to_row(col):
    return jnp.sum(jnp.where(eye(), jnp.broadcast_to(col, (F, F)), 0.0), axis=0, keepdims=True)


def wide(row):
    return jnp.broadcast_to(to_col(row), (F, 128))


class Group:
    def __init__(self, n, me, target, send, recv):
        self.n, self.me, self.target, self.send, self.recv = n, me, target, send, recv

    def peers(self):
        return [lax.rem(self.me + d, self.n) for d in range(1, self.n)]

    def copy(self, src, dst, p):
        return pltpu.make_async_remote_copy(
            src_ref=src, dst_ref=dst, send_sem=self.send, recv_sem=self.recv,
            device_id=self.target(p), device_id_type=MESH,
        )

    def spread(self, buf):
        for p in self.peers():
            self.copy(buf.at[self.me], buf.at[self.me], p).start()

    def scatter(self, src, buf):
        for p in self.peers():
            self.copy(src.at[p], buf.at[self.me], p).start()

    def all_bytes(self, buf):
        rest = buf.at[pl.ds(0, self.n - 1)]
        return self.copy(rest, rest, self.me)

    def arrive(self, buf):
        if self.n > 1:
            self.all_bytes(buf).wait_recv()

    def done(self, buf):
        if self.n > 1:
            self.all_bytes(buf).wait_send()


def kernel(
    dims,
    x_ref, lab_ref, wt_ref, bt_ref, wf_ref, gam_ref, bet_ref, wh_ref, bh_ref,
    gr_ref, gwt_ref, gwf_ref, vec_ref,
    wts, wtt, wfb, wfr, xcol, dcol, h1, sl1, z2, sl2, dz2, dz1, par, acc, accr, lab, dl, dll, dlr,
    gt, gt2,
    sp1, sz1, sp2, sz2,
    ga, ra, za, fa, gb, rb, zb, fb,
    hs, hr, ds, dr, sem,
):
    nf, nx, nz, C, T = dims
    total = float(nf * nx * nz * C * T)
    cells = float(nf * C * T)
    fi = lax.axis_index("fibre")
    ri = lax.axis_index("record")
    xi, zi = ri // nz, lax.rem(ri, nz)

    def plane(i):
        return Group(
            nf * nx, fi * nx + xi, lambda p: (p // nx, lax.rem(p, nx) * nz + zi), sem.at[2 * i], sem.at[2 * i + 1]
        )

    def line(i):
        return Group(nz, zi, lambda p: (fi, xi * nz + p), sem.at[2 * i], sem.at[2 * i + 1])

    barrier = pltpu.get_barrier_semaphore()
    for group in (plane(0), line(1)):
        for p in group.peers():
            pl.semaphore_signal(barrier, inc=1, device_id=group.target(p), device_id_type=MESH)

    for k in range(TAPS):
        wts[:, k * F:(k + 1) * F] = wt_ref[k]
        wtt[:, k * F:(k + 1) * F] = wt_ref[k].astype(F32).T.astype(BF)
    wfb[...] = jnp.zeros_like(wfb)
    wfr[...] = jnp.zeros_like(wfr)
    for k in range(TAPS):
        w = wf_ref[k]
        wr = wf_ref[TAPS - 1 - k].astype(F32).T.astype(BF)
        for j in range(4):
            wfb[j * F:(j + 1) * F, (j + k) * F:(j + k + 1) * F] = w
            wfr[j * F:(j + 1) * F, (j + k) * F:(j + k + 1) * F] = wr
    for c in range(C):
        lab[c] = lab_ref[c:c + 1, :].astype(F32)
    par[0] = wide(bt_ref[...])
    acc[...] = jnp.zeros_like(acc)
    accr[...] = jnp.zeros_like(accr)

    has_l, has_r = fi > 0, fi < nf - 1
    left, right = lax.rem(fi + nf - 1, nf), lax.rem(fi + 1, nf)

    @pl.when(jnp.logical_not(has_l))
    def _():
        for i in range(2 * HALF):
            h1[i] = jnp.zeros((F, T), BF)
        for i in range(HALF):
            dz2[i] = jnp.zeros((F, T), BF)

    @pl.when(jnp.logical_not(has_r))
    def _():
        for i in range(2 * HALF):
            h1[2 * HALF + C + i] = jnp.zeros((F, T), BF)
        for i in range(HALF):
            dz2[HALF + C + i] = jnp.zeros((F, T), BF)

    def halo(c, side):
        slot = c + 2 * HALF + C if side == "l" else c + 2 * HALF - C
        index = c + 2 * HALF if side == "l" else c + 2 * HALF - C
        return pltpu.make_async_remote_copy(
            src_ref=h1.at[c + 2 * HALF],
            dst_ref=h1.at[slot],
            send_sem=hs.at[index],
            recv_sem=hr.at[index],
            device_id=(left if side == "l" else right, ri),
            device_id_type=MESH,
        )

    def halo_arrive(i, side):
        slot = i if side == "l" else i + 2 * HALF + C
        index = i if side == "l" else i + 2 * HALF
        pltpu.make_async_remote_copy(
            src_ref=h1.at[slot], dst_ref=h1.at[slot], send_sem=hs.at[index], recv_sem=hr.at[index],
            device_id=(left if side == "l" else right, ri), device_id_type=MESH,
        ).wait_recv()

    lane = lax.broadcasted_iota(jnp.int32, (F, 128), 1)

    def shifted(src, dst, sign):
        for k in range(TAPS):
            s = sign * DILATION * (k - HALF)
            rows = slice(k * F, (k + 1) * F)
            if s == 0:
                dst[rows, :] = src.astype(BF)
                continue
            r = pltpu.roll(src, (-s) % T, 1)
            dst[rows, :] = r.astype(BF)
            if s > 0:
                dst[rows, T - 128:] = jnp.where(lane < 128 - s, r[:, T - 128:], jnp.zeros((), r.dtype)).astype(BF)
            else:
                dst[rows, :128] = jnp.where(lane >= -s, r[:, :128], jnp.zeros((), r.dtype)).astype(BF)

    def forward(i, carry):
        c = jnp.where(lax.rem(i, 2) == 0, i // 2, C - 1 - i // 2)
        shifted(x_ref[c], xcol.at[c], 1)
        for n in range(0, T, 256):
            pre2 = mm(wts[...], xcol[c, :, n:n + 256])
            for m in range(0, 256, 128):
                cols = slice(n + m, n + m + 128)
                pre = pre2[:, m:m + 128] + par[0]
                s = sigmoid(pre)
                h = pre * s
                h1[c + 2 * HALF, :, cols] = h.astype(BF)
                sl1[c, :, cols] = s + h * (1.0 - s)

        return carry

    def forward_send(i, carry):
        c = jnp.where(lax.rem(i, 2) == 0, i // 2, C - 1 - i // 2)
        forward(i, carry)

        @pl.when(jnp.logical_and(has_l, c < HALF))
        def _():
            halo(c, "l").start()

        @pl.when(jnp.logical_and(has_r, c >= C - HALF))
        def _():
            halo(c, "r").start()

        return carry

    lax.fori_loop(0, 2, forward, 0)
    pl.semaphore_wait(barrier, nf * nx + nz - 2)

    @pl.when(has_l)
    def _():
        halo(0, "l").start()

    @pl.when(has_r)
    def _():
        halo(C - 1, "r").start()

    lax.fori_loop(2, C, forward_send, 0)
    for d in range(HALF):
        @pl.when(has_l)
        def _():
            halo(HALF + d, "l").start()

        @pl.when(has_r)
        def _():
            halo(C - HALF - 1 - d, "r").start()

    def fibre_conv(first, count, lo):
        def body(n, carry):
            cols = pl.ds(pl.multiple_of(n * 256, 256), 256)
            data = h1[lo:lo + count + 2 * HALF, :, cols].reshape((count + 2 * HALF) * F, 256)
            out = mm(wfb[:count * F, :(count + 2 * HALF) * F], data)
            z2[first:first + count, :, cols] = out.reshape(count, F, 256)
            return carry

        lax.fori_loop(0, T // 256, body, 0)

    @pl.when(has_l)
    def _():
        for i in range(HALF):
            halo_arrive(HALF + i, "l")

    fibre_conv(HALF, 4, HALF)

    @pl.when(has_r)
    def _():
        for i in range(HALF):
            halo_arrive(i, "r")

    fibre_conv(HALF + 4, 4, HALF + 4)

    def add_up(c, total_):
        for n in range(0, T, 128):
            total_ = total_ + z2[HALF + c, :, n:n + 128]
        return total_

    zero = jnp.zeros((F, 128), F32)
    own_mean = jnp.sum(lax.fori_loop(0, C, add_up, zero), axis=1, keepdims=True) / float(C * T)
    own_wide = jnp.broadcast_to(own_mean, (F, 128))

    def spread_up(c, total_):
        for n in range(0, T, 128):
            d = z2[HALF + c, :, n:n + 128] - own_wide
            total_ = total_ + d * d
        return total_

    own_m2 = jnp.sum(lax.fori_loop(0, C, spread_up, zero), axis=1, keepdims=True)

    def merge(buf, n, count):
        value = buf[...]
        total_ = jnp.sum(value, axis=0)
        d = value - total_[None] * (1.0 / n)
        m2 = jnp.sum(d * d, axis=0) * count
        return jnp.concatenate([total_[:, :F] * (1.0 / n), total_[:, F:] + m2[:, :F]], axis=1)

    def plain(buf):
        return jnp.sum(buf[...], axis=0)

    p1, z1 = plane(0), line(1)
    sp1[p1.me] = jnp.concatenate([to_row(own_mean), to_row(own_m2)], axis=1)
    p1.spread(sp1)

    @pl.when(has_l)
    def _():
        for i in range(HALF):
            halo_arrive(i, "l")
        fibre_conv(0, HALF, 0)

    p1.arrive(sp1)
    sz1[zi] = merge(sp1, nf * nx, float(C * T))
    z1.spread(sz1)

    @pl.when(has_r)
    def _():
        for i in range(HALF):
            halo_arrive(HALF + i, "r")
        fibre_conv(HALF + C, HALF, HALF + C)

    z1.arrive(sz1)
    stats = merge(sz1, nz, float(C * T * nf * nx))
    mean_row = stats[:, :F]
    rstd_row = lax.rsqrt(stats[:, F:] / total + EPS)
    par[1] = wide(mean_row)
    par[2] = wide(gam_ref[...] * rstd_row)
    par[3] = wide(bet_ref[...])
    par[4] = wide(wh_ref[...].astype(F32))
    par[5] = wide(rstd_row)

    bias = bh_ref[0, 0]

    def head(c, carry):
        for n in range(0, T, 128):
            cols = slice(n, n + 128)
            zc = z2[HALF + c, :, cols] - par[1]
            act = zc * par[2] + par[3]
            s = sigmoid(act)
            h = act * s
            h2 = h.astype(BF).astype(F32)
            logit = jnp.sum(h2 * par[4], axis=0, keepdims=True) + bias
            target = lab[c, :, cols]
            soft = jnp.maximum(logit, 0.0) + jnp.log1p(jnp.exp(-jnp.abs(logit)))
            accr[0:1, :] += soft - target * logit
            dlogit = sigmoid(logit) - target
            dl[c, :, cols] = dlogit
            dh2 = (dlogit * par[4]).astype(BF).astype(F32)
            dact = dh2 * (s + h * (1.0 - s))
            sl2[HALF + c, :, cols] = dact
            acc[0] += dact
            acc[1] += dact * zc
            acc[2] += dlogit * h2
        return carry

    lax.fori_loop(0, C, head, 0)

    def dl_copy(side):
        i = 0 if side == "l" else 1
        return pltpu.make_async_remote_copy(
            src_ref=dl.at[0:HALF] if side == "l" else dl.at[C - HALF:C], dst_ref=dlr if side == "l" else dll, send_sem=ds.at[i], recv_sem=dr.at[i],
            device_id=(left if side == "l" else right, ri), device_id_type=MESH,
        )

    def dl_arrive(side):
        i = 1 if side == "l" else 0
        buf = dll if side == "l" else dlr
        pltpu.make_async_remote_copy(
            src_ref=buf, dst_ref=buf, send_sem=ds.at[i], recv_sem=dr.at[i],
            device_id=(left if side == "l" else right, ri), device_id_type=MESH,
        ).wait_recv()

    @pl.when(has_l)
    def _():
        dl_copy("l").start()

    @pl.when(has_r)
    def _():
        dl_copy("r").start()

    def lanes(v):
        return jnp.sum(v, axis=1, keepdims=True)

    p2, z2_ = plane(2), line(3)
    sp2[p2.me] = jnp.concatenate([to_row(lanes(acc[0])), to_row(lanes(acc[1]))], axis=1)
    p2.spread(sp2)

    def halo_dact(slot, buf, row):
        for n in range(0, T, 128):
            cols = slice(n, n + 128)
            act = (z2[slot, :, cols] - par[1]) * par[2] + par[3]
            s = sigmoid(act)
            dh2 = (buf[row, :, cols] * par[4]).astype(BF).astype(F32)
            sl2[slot, :, cols] = dh2 * (s + act * s * (1.0 - s))

    def halo_left(i, carry):
        halo_dact(i, dll, i)
        return carry

    def halo_right(i, carry):
        halo_dact(HALF + C + i, dlr, i)
        return carry

    @pl.when(has_l)
    def _():
        dl_arrive("l")
        lax.fori_loop(0, HALF, halo_left, 0)

    p2.arrive(sp2)
    sz2[zi] = plain(sp2)
    z2_.spread(sz2)

    @pl.when(has_r)
    def _():
        dl_arrive("r")
        lax.fori_loop(0, HALF, halo_right, 0)

    z2_.arrive(sz2)
    sums = plain(sz2)
    rstd_row = to_row(par[5][:, 0:1])
    beta_row = sums[:, :F]
    gamma_row = sums[:, F:] * rstd_row
    vec_ref[2:3, :F] = beta_row / cells
    vec_ref[1:2, :F] = gamma_row / cells
    par[6] = wide(beta_row / total)
    par[7] = wide(gamma_row * rstd_row / total)

    def slope_back(slot, carry):
        for n in range(0, T, 128):
            cols = slice(n, n + 128)
            zc = z2[slot, :, cols] - par[1]
            dz2[slot, :, cols] = (par[2] * (sl2[slot, :, cols] - par[6] - zc * par[7])).astype(BF)
        return carry

    lax.fori_loop(jnp.where(has_l, 0, HALF), jnp.where(has_r, C + 2 * HALF, C + HALF), slope_back, 0)

    for q in range(2):
        grad = lax.dot_general(
            dz2[HALF + 4 * q:HALF + 4 * q + 4].reshape(4 * F, T),
            h1[HALF + 4 * q:HALF + 4 * q + 10].reshape(10 * F, T),
            NT, preferred_element_type=F32,
        )
        for j in range(4):
            piece = grad[j * F:(j + 1) * F, j * F:(j + TAPS) * F]
            if q == 0 and j == 0:
                gt[:, :TAPS * F] = piece
            else:
                gt[:, :TAPS * F] += piece
    col = lax.broadcasted_iota(jnp.int32, (F, F), 1)

    rows, width = F // nf, 512 // nx

    def pack(src, dst, first, second):
        src[:, TAPS * F:] = jnp.where(col == 0, jnp.broadcast_to(first, (F, F)), jnp.where(col == 1, jnp.broadcast_to(second, (F, F)), 0.0))
        for p in range(nf):
            for q in range(nx):
                dst[p * nx + q] = src[p * rows:(p + 1) * rows, q * width:(q + 1) * width]

    loss_part = jnp.sum(accr[0:1, :], axis=1, keepdims=True)
    pack(gt, ga, lanes(acc[2]), jnp.where(lax.broadcasted_iota(jnp.int32, (F, 1), 0) == 0, jnp.broadcast_to(loss_part, (F, 1)), 0.0))
    a1, a2, a3 = plane(4), line(5), plane(6)
    b1, b2, b3 = plane(7), line(8), plane(9)
    a1.scatter(ga, ra)
    ra[a1.me] = ga[a1.me]

    def fibre_back(q):
        def body(n, carry):
            cols = pl.ds(pl.multiple_of(n * 256, 256), 256)
            data = dz2[4 * q:4 * q + 10, :, cols].reshape(10 * F, 256)
            out = mm(wfr[...], data).reshape(4, F, 256)
            for j in range(4):
                dh = out[j].astype(BF).astype(F32)
                value = (dh * sl1[4 * q + j, :, cols]).astype(BF)
                dz1[4 * q + j, :, cols] = value
                value = value.astype(F32)
                acc[3] += value[:, :128] + value[:, 128:]
            return carry

        lax.fori_loop(0, T // 256, body, 0)

    fibre_back(0)
    fibre_back(1)
    a1.arrive(ra)
    za[zi] = plain(ra)
    a2.spread(za)
    gt2[...] = jnp.zeros_like(gt2)

    def time_grad(c, carry):
        gt2[...] += lax.dot_general(xcol[c], dz1[c], NT, preferred_element_type=F32)
        return carry

    lax.fori_loop(0, C, time_grad, 0)
    for k in range(TAPS):
        gt[:, k * F:(k + 1) * F] = gt2[k * F:(k + 1) * F, :].T
    pack(gt, gb, lanes(acc[3]), jnp.zeros((F, 1), F32))
    b1.scatter(gb, rb)
    rb[b1.me] = gb[b1.me]
    a2.arrive(za)
    fa[a3.me] = plain(za)
    a3.spread(fa)
    def time_back(c, carry):
        shifted(dz1[c], dcol, -1)
        for n in range(0, T, 256):
            gr_ref[c, :, n:n + 256] = mm(wtt[...], dcol[:, n:n + 256]).astype(BF)
        return carry

    lax.fori_loop(0, 4, time_back, 0)
    b1.arrive(rb)
    zb[zi] = plain(rb)
    b2.spread(zb)
    lax.fori_loop(4, C, time_back, 0)
    b2.arrive(zb)
    fb[b3.me] = plain(zb)
    b3.spread(fb)

    def unpack(buf, out):
        whole = jnp.concatenate(
            [jnp.concatenate([buf[p * nx + q] for q in range(nx)], axis=1) for p in range(nf)], axis=0
        )
        value = whole / cells
        for k in range(TAPS):
            out[k] = value[:, k * F:(k + 1) * F]
        return whole[:, TAPS * F:]

    a3.arrive(fa)
    tail = unpack(fa, gwf_ref)
    vec_ref[3:4, :F] = to_row(tail[:, 0:1] / cells)
    vec_ref[4:5, :F] = jnp.broadcast_to(tail[0:1, 1:2] / total, (1, F))
    b3.arrive(fb)
    tail = unpack(fb, gwt_ref)
    vec_ref[0:1, :F] = to_row(tail[:, 0:1] / cells)

    for group, buf in (
        (p1, sp1), (z1, sz1), (p2, sp2), (z2_, sz2),
        (a1, ga), (a2, za), (a3, fa), (b1, gb), (b2, zb), (b3, fb),
    ):
        group.done(buf)

    @pl.when(has_l)
    def _():
        dl_copy("l").wait_send()
        for c in range(2 * HALF):
            halo(c, "l").wait_send()

    @pl.when(has_r)
    def _():
        dl_copy("r").wait_send()
        for c in range(2 * HALF):
            halo(C - 1 - c, "r").wait_send()


def hand_out(gr, gwt, gwf, vec, gr_ref, gwt_ref, gbt_ref, gwf_ref, gga_ref, gbe_ref, gwh_ref, loss_ref, sem):
    copies = [
        pltpu.make_async_copy(a, b, sem.at[i])
        for i, (a, b) in enumerate(((gr, gr_ref), (gwt, gwt_ref), (gwf, gwf_ref)))
    ]
    for copy in copies:
        copy.start()
    for i, ref in enumerate((gbt_ref, gga_ref, gbe_ref, gwh_ref)):
        ref[...] = vec[i:i + 1, :F]
    loss_ref[...] = vec[4:5, 0:1]
    for copy in copies:
        copy.wait()


def local(dims, records, labels, w_time, b_time, w_fibre, gamma, beta, w_head, b_head):
    nf, nx, nz, C, T = dims
    vm = pl.BlockSpec(memory_space=pltpu.VMEM)
    anywhere = pl.BlockSpec(memory_space=pl.ANY)
    S = jax.ShapeDtypeStruct
    V = pltpu.VMEM
    D = pltpu.SemaphoreType.DMA
    n = nf * nx
    rows, width = F // nf, 512 // nx

    def large():
        return [V((n, rows, width), F32), V((n, rows, width), F32), V((nz, rows, width), F32), V((n, rows, width), F32)]

    gr, gwt, gwf, vec = pl.pallas_call(
        functools.partial(kernel, dims),
        out_shape=(S((C, F, T), BF), S((TAPS, F, F), F32), S((TAPS, F, F), F32), S((8, 128), F32)),
        in_specs=[vm] * 8 + [pl.BlockSpec(memory_space=pltpu.SMEM)],
        out_specs=[vm] * 4,
        scratch_shapes=[
            V((F, TAPS * F), BF), V((F, TAPS * F), BF), V((4 * F, 10 * F), BF), V((4 * F, 10 * F), BF),
            V((C, TAPS * F, T), BF), V((TAPS * F, T), BF), V((C + 12, F, T), BF), V((C, F, T), F32),
            V((C + 6, F, T), F32), V((C + 6, F, T), F32), V((C + 6, F, T), BF), V((C, F, T), BF),
            V((8, F, 128), F32), V((4, F, 128), F32), V((8, 128), F32),
            V((C, 1, T), F32), V((C, 1, T), F32), V((HALF, 1, T), F32), V((HALF, 1, T), F32),
            V((F, 512), F32), V((TAPS * F, F), F32),
            V((n, 1, 128), F32), V((nz, 1, 128), F32), V((n, 1, 128), F32), V((nz, 1, 128), F32),
            *large(), *large(),
            D((12,)), D((12,)), D((2,)), D((2,)), D((20,)),
        ],
        compiler_params=pltpu.CompilerParams(
            collective_id=0, has_side_effects=True, vmem_limit_bytes=56 * 1024 * 1024
        ),
    )(
        records[0], labels[0], w_time, b_time.reshape(1, F), w_fibre, gamma.reshape(1, F), beta.reshape(1, F),
        w_head.reshape(1, F), b_head.reshape(1, 1),
    )
    row = S((1, F), F32)
    gr, gwt, gbt, gwf, gga, gbe, gwh, loss = pl.pallas_call(
        hand_out,
        out_shape=(S((C, F, T), BF), S((TAPS, F, F), F32), row, S((TAPS, F, F), F32), row, row, row, S((1, 1), F32)),
        in_specs=[vm] * 4,
        out_specs=[anywhere, anywhere, vm, anywhere] + [vm] * 4,
        scratch_shapes=[D((3,))],
        compiler_params=pltpu.CompilerParams(vmem_limit_bytes=60 * 1024 * 1024),
    )(gr, gwt, gwf, vec)
    return gr[None], gwt, gbt[0], gwf, gga[0], gbe[0], gwh[0], loss[0, 0]


def solution(mesh):
    nf, nr = mesh.shape["fibre"], mesh.shape["record"]
    nx = 4 if nr % 4 == 0 else 1

    def run(records, *rest):
        dims = (nf, nx, nr // nx, records.shape[1] // nf, records.shape[3])
        return jax.shard_map(
            functools.partial(local, dims),
            mesh=mesh,
            in_specs=(P("record", "fibre", None, None), P("record", "fibre", None)) + (P(),) * 7,
            out_specs=(P("record", "fibre", None, None),) + (P(),) * 7,
            check_vma=False,
        )(records, *rest)

    return run
```

```python
import functools

import jax
import jax.numpy as jnp
from jax import lax
from jax.experimental import pallas as pl
from jax.experimental.pallas import tpu as pltpu
from jax.sharding import PartitionSpec as P

F = 64
TAPS = 7
DILATION = 2
HALF = 3
EPS = 1e-05
BF = jnp.bfloat16
F32 = jnp.float32
MESH = pl.DeviceIdType.MESH
NT = (((1,), (1,)), ((), ()))


def mm(a, b):
    return jnp.dot(a, b, preferred_element_type=F32)


def sigmoid(v):
    return 0.5 * jnp.tanh(0.5 * v) + 0.5


def eye():
    return lax.broadcasted_iota(jnp.int32, (F, F), 0) == lax.broadcasted_iota(jnp.int32, (F, F), 1)


def to_col(row):
    return jnp.sum(jnp.where(eye(), jnp.broadcast_to(row, (F, F)), 0.0), axis=1, keepdims=True)


def to_row(col):
    return jnp.sum(jnp.where(eye(), jnp.broadcast_to(col, (F, F)), 0.0), axis=0, keepdims=True)


def wide(row):
    return jnp.broadcast_to(to_col(row), (F, 128))


class Group:
    def __init__(self, n, me, target, send, recv):
        self.n, self.me, self.target, self.send, self.recv = n, me, target, send, recv

    def peers(self):
        return [lax.rem(self.me + d, self.n) for d in range(1, self.n)]

    def copy(self, src, dst, p):
        return pltpu.make_async_remote_copy(
            src_ref=src, dst_ref=dst, send_sem=self.send, recv_sem=self.recv,
            device_id=self.target(p), device_id_type=MESH,
        )

    def spread(self, buf):
        for p in self.peers():
            self.copy(buf.at[self.me], buf.at[self.me], p).start()

    def scatter(self, src, buf):
        for p in self.peers():
            self.copy(src.at[p], buf.at[self.me], p).start()

    def all_bytes(self, buf):
        rest = buf.at[pl.ds(0, self.n - 1)]
        return self.copy(rest, rest, self.me)

    def arrive(self, buf):
        if self.n > 1:
            self.all_bytes(buf).wait_recv()

    def done(self, buf):
        if self.n > 1:
            self.all_bytes(buf).wait_send()


def kernel(
    dims,
    x_ref, lab_ref, wt_ref, bt_ref, wf_ref, gam_ref, bet_ref, wh_ref, bh_ref,
    gr_ref, gwt_ref, gwf_ref, vec_ref,
    wts, wtt, wfb, wfr, xcol, dcol, h1, sl1, z2, sl2, dz2, dz1, par, acc, accr, lab, dl, dll, dlr,
    gt, gt2,
    sp1, sz1, sp2, sz2,
    ga, ra, za, fa, gb, rb, zb, fb,
    hs, hr, ds, dr, sem,
):
    nf, nx, nz, C, T = dims
    total = float(nf * nx * nz * C * T)
    cells = float(nf * C * T)
    fi = lax.axis_index("fibre")
    ri = lax.axis_index("record")
    xi, zi = ri // nz, lax.rem(ri, nz)

    def plane(i):
        return Group(
            nf * nx, fi * nx + xi, lambda p: (p // nx, lax.rem(p, nx) * nz + zi), sem.at[2 * i], sem.at[2 * i + 1]
        )

    def line(i):
        return Group(nz, zi, lambda p: (fi, xi * nz + p), sem.at[2 * i], sem.at[2 * i + 1])

    barrier = pltpu.get_barrier_semaphore()
    for group in (plane(0), line(1)):
        for p in group.peers():
            pl.semaphore_signal(barrier, inc=1, device_id=group.target(p), device_id_type=MESH)

    for k in range(TAPS):
        wts[:, k * F:(k + 1) * F] = wt_ref[k]
        wtt[:, k * F:(k + 1) * F] = wt_ref[k].astype(F32).T.astype(BF)
    wfb[...] = jnp.zeros_like(wfb)
    wfr[...] = jnp.zeros_like(wfr)
    for k in range(TAPS):
        w = wf_ref[k]
        wr = wf_ref[TAPS - 1 - k].astype(F32).T.astype(BF)
        for j in range(4):
            wfb[j * F:(j + 1) * F, (j + k) * F:(j + k + 1) * F] = w
            wfr[j * F:(j + 1) * F, (j + k) * F:(j + k + 1) * F] = wr
    for c in range(C):
        lab[c] = lab_ref[c:c + 1, :].astype(F32)
    par[0] = wide(bt_ref[...])
    acc[...] = jnp.zeros_like(acc)
    accr[...] = jnp.zeros_like(accr)

    has_l, has_r = fi > 0, fi < nf - 1
    left, right = lax.rem(fi + nf - 1, nf), lax.rem(fi + 1, nf)

    @pl.when(jnp.logical_not(has_l))
    def _():
        for i in range(2 * HALF):
            h1[i] = jnp.zeros((F, T), BF)
        for i in range(HALF):
            dz2[i] = jnp.zeros((F, T), BF)

    @pl.when(jnp.logical_not(has_r))
    def _():
        for i in range(2 * HALF):
            h1[2 * HALF + C + i] = jnp.zeros((F, T), BF)
        for i in range(HALF):
            dz2[HALF + C + i] = jnp.zeros((F, T), BF)

    def halo(c, side):
        slot = c + 2 * HALF + C if side == "l" else c + 2 * HALF - C
        index = c + 2 * HALF if side == "l" else c + 2 * HALF - C
        return pltpu.make_async_remote_copy(
            src_ref=h1.at[c + 2 * HALF],
            dst_ref=h1.at[slot],
            send_sem=hs.at[index],
            recv_sem=hr.at[index],
            device_id=(left if side == "l" else right, ri),
            device_id_type=MESH,
        )

    def halo_arrive(i, side):
        slot = i if side == "l" else i + 2 * HALF + C
        index = i if side == "l" else i + 2 * HALF
        pltpu.make_async_remote_copy(
            src_ref=h1.at[slot], dst_ref=h1.at[slot], send_sem=hs.at[index], recv_sem=hr.at[index],
            device_id=(left if side == "l" else right, ri), device_id_type=MESH,
        ).wait_recv()

    lane = lax.broadcasted_iota(jnp.int32, (F, 128), 1)

    def shifted(src, dst, sign):
        for k in range(TAPS):
            s = sign * DILATION * (k - HALF)
            rows = slice(k * F, (k + 1) * F)
            if s == 0:
                dst[rows, :] = src.astype(BF)
                continue
            r = pltpu.roll(src, (-s) % T, 1)
            dst[rows, :] = r.astype(BF)
            if s > 0:
                dst[rows, T - 128:] = jnp.where(lane < 128 - s, r[:, T - 128:], jnp.zeros((), r.dtype)).astype(BF)
            else:
                dst[rows, :128] = jnp.where(lane >= -s, r[:, :128], jnp.zeros((), r.dtype)).astype(BF)

    def forward(i, carry):
        c = jnp.where(lax.rem(i, 2) == 0, i // 2, C - 1 - i // 2)
        shifted(x_ref[c], xcol.at[c], 1)
        for n in range(0, T, 256):
            pre2 = mm(wts[...], xcol[c, :, n:n + 256])
            for m in range(0, 256, 128):
                cols = slice(n + m, n + m + 128)
                pre = pre2[:, m:m + 128] + par[0]
                s = sigmoid(pre)
                h = pre * s
                h1[c + 2 * HALF, :, cols] = h.astype(BF)
                sl1[c, :, cols] = s + h * (1.0 - s)

        return carry

    def forward_send(i, carry):
        c = jnp.where(lax.rem(i, 2) == 0, i // 2, C - 1 - i // 2)
        forward(i, carry)

        @pl.when(jnp.logical_and(has_l, c < HALF))
        def _():
            halo(c, "l").start()

        @pl.when(jnp.logical_and(has_r, c >= C - HALF))
        def _():
            halo(c, "r").start()

        return carry

    lax.fori_loop(0, 2, forward, 0, unroll=2)
    pl.semaphore_wait(barrier, nf * nx + nz - 2)

    @pl.when(has_l)
    def _():
        halo(0, "l").start()

    @pl.when(has_r)
    def _():
        halo(C - 1, "r").start()

    lax.fori_loop(2, C, forward_send, 0, unroll=6)
    for d in range(HALF):
        @pl.when(has_l)
        def _():
            halo(HALF + d, "l").start()

        @pl.when(has_r)
        def _():
            halo(C - HALF - 1 - d, "r").start()

    def fibre_conv(first, count, lo):
        def body(n, carry):
            cols = pl.ds(pl.multiple_of(n * 256, 256), 256)
            data = h1[lo:lo + count + 2 * HALF, :, cols].reshape((count + 2 * HALF) * F, 256)
            out = mm(wfb[:count * F, :(count + 2 * HALF) * F], data)
            z2[first:first + count, :, cols] = out.reshape(count, F, 256)
            return carry

        lax.fori_loop(0, T // 256, body, 0, unroll=4)

    @pl.when(has_l)
    def _():
        for i in range(HALF):
            halo_arrive(HALF + i, "l")

    fibre_conv(HALF, 4, HALF)

    @pl.when(has_r)
    def _():
        for i in range(HALF):
            halo_arrive(i, "r")

    fibre_conv(HALF + 4, 4, HALF + 4)

    def add_up(c, total_):
        for n in range(0, T, 128):
            total_ = total_ + z2[HALF + c, :, n:n + 128]
        return total_

    zero = jnp.zeros((F, 128), F32)
    own_mean = jnp.sum(lax.fori_loop(0, C, add_up, zero), axis=1, keepdims=True) / float(C * T)
    own_wide = jnp.broadcast_to(own_mean, (F, 128))

    def spread_up(c, total_):
        for n in range(0, T, 128):
            d = z2[HALF + c, :, n:n + 128] - own_wide
            total_ = total_ + d * d
        return total_

    own_m2 = jnp.sum(lax.fori_loop(0, C, spread_up, zero), axis=1, keepdims=True)

    def merge(buf, n, count):
        value = buf[...]
        total_ = jnp.sum(value, axis=0)
        d = value - total_[None] * (1.0 / n)
        m2 = jnp.sum(d * d, axis=0) * count
        return jnp.concatenate([total_[:, :F] * (1.0 / n), total_[:, F:] + m2[:, :F]], axis=1)

    def plain(buf):
        return jnp.sum(buf[...], axis=0)

    p1, z1 = plane(0), line(1)
    sp1[p1.me] = jnp.concatenate([to_row(own_mean), to_row(own_m2)], axis=1)
    p1.spread(sp1)

    p1.arrive(sp1)
    sz1[zi] = merge(sp1, nf * nx, float(C * T))
    z1.spread(sz1)

    @pl.when(has_l)
    def _():
        for i in range(HALF):
            halo_arrive(i, "l")
        fibre_conv(0, HALF, 0)

    @pl.when(has_r)
    def _():
        for i in range(HALF):
            halo_arrive(HALF + i, "r")
        fibre_conv(HALF + C, HALF, HALF + C)

    z1.arrive(sz1)
    stats = merge(sz1, nz, float(C * T * nf * nx))
    mean_row = stats[:, :F]
    rstd_row = lax.rsqrt(stats[:, F:] / total + EPS)
    par[1] = wide(mean_row)
    par[2] = wide(gam_ref[...] * rstd_row)
    par[3] = wide(bet_ref[...])
    par[4] = wide(wh_ref[...].astype(F32))
    par[5] = wide(rstd_row)

    bias = bh_ref[0, 0]

    def head(c, carry):
        for n in range(0, T, 128):
            cols = slice(n, n + 128)
            zc = z2[HALF + c, :, cols] - par[1]
            act = zc * par[2] + par[3]
            s = sigmoid(act)
            h = act * s
            h2 = h.astype(BF).astype(F32)
            logit = jnp.sum(h2 * par[4], axis=0, keepdims=True) + bias
            target = lab[c, :, cols]
            soft = jnp.maximum(logit, 0.0) + jnp.log1p(jnp.exp(-jnp.abs(logit)))
            accr[0:1, :] += soft - target * logit
            dlogit = sigmoid(logit) - target
            dl[c, :, cols] = dlogit
            dh2 = (dlogit * par[4]).astype(BF).astype(F32)
            dact = dh2 * (s + h * (1.0 - s))
            sl2[HALF + c, :, cols] = dact
            acc[0] += dact
            acc[1] += dact * zc
            acc[2] += dlogit * h2
        return carry

    lax.fori_loop(0, C, head, 0, unroll=4)

    def dl_copy(side):
        i = 0 if side == "l" else 1
        return pltpu.make_async_remote_copy(
            src_ref=dl.at[0:HALF] if side == "l" else dl.at[C - HALF:C], dst_ref=dlr if side == "l" else dll, send_sem=ds.at[i], recv_sem=dr.at[i],
            device_id=(left if side == "l" else right, ri), device_id_type=MESH,
        )

    def dl_arrive(side):
        i = 1 if side == "l" else 0
        buf = dll if side == "l" else dlr
        pltpu.make_async_remote_copy(
            src_ref=buf, dst_ref=buf, send_sem=ds.at[i], recv_sem=dr.at[i],
            device_id=(left if side == "l" else right, ri), device_id_type=MESH,
        ).wait_recv()

    @pl.when(has_l)
    def _():
        dl_copy("l").start()

    @pl.when(has_r)
    def _():
        dl_copy("r").start()

    def lanes(v):
        return jnp.sum(v, axis=1, keepdims=True)

    p2, z2_ = plane(2), line(3)
    sp2[p2.me] = jnp.concatenate([to_row(lanes(acc[0])), to_row(lanes(acc[1]))], axis=1)
    p2.spread(sp2)

    def halo_dact(slot, buf, row):
        for n in range(0, T, 128):
            cols = slice(n, n + 128)
            act = (z2[slot, :, cols] - par[1]) * par[2] + par[3]
            s = sigmoid(act)
            dh2 = (buf[row, :, cols] * par[4]).astype(BF).astype(F32)
            sl2[slot, :, cols] = dh2 * (s + act * s * (1.0 - s))

    def halo_left(i, carry):
        halo_dact(i, dll, i)
        return carry

    def halo_right(i, carry):
        halo_dact(HALF + C + i, dlr, i)
        return carry

    @pl.when(has_l)
    def _():
        dl_arrive("l")
        lax.fori_loop(0, HALF, halo_left, 0)

    p2.arrive(sp2)
    sz2[zi] = plain(sp2)
    z2_.spread(sz2)

    @pl.when(has_r)
    def _():
        dl_arrive("r")
        lax.fori_loop(0, HALF, halo_right, 0)

    z2_.arrive(sz2)
    sums = plain(sz2)
    rstd_row = to_row(par[5][:, 0:1])
    beta_row = sums[:, :F]
    gamma_row = sums[:, F:] * rstd_row
    vec_ref[2:3, :F] = beta_row / cells
    vec_ref[1:2, :F] = gamma_row / cells
    par[6] = wide(beta_row / total)
    par[7] = wide(gamma_row * rstd_row / total)

    def slope_back(slot, carry):
        for n in range(0, T, 128):
            cols = slice(n, n + 128)
            zc = z2[slot, :, cols] - par[1]
            dz2[slot, :, cols] = (par[2] * (sl2[slot, :, cols] - par[6] - zc * par[7])).astype(BF)
        return carry

    lax.fori_loop(HALF, HALF + C, slope_back, 0, unroll=2)

    @pl.when(has_l)
    def _():
        lax.fori_loop(0, HALF, slope_back, 0)

    @pl.when(has_r)
    def _():
        lax.fori_loop(C + HALF, C + 2 * HALF, slope_back, 0)


    for q in range(2):
        grad = lax.dot_general(
            dz2[HALF + 4 * q:HALF + 4 * q + 4].reshape(4 * F, T),
            h1[HALF + 4 * q:HALF + 4 * q + 10].reshape(10 * F, T),
            NT, preferred_element_type=F32,
        )
        for j in range(4):
            piece = grad[j * F:(j + 1) * F, j * F:(j + TAPS) * F]
            if q == 0 and j == 0:
                gt[:, :TAPS * F] = piece
            else:
                gt[:, :TAPS * F] += piece
    col = lax.broadcasted_iota(jnp.int32, (F, F), 1)

    rows, width = F // nf, 512 // nx

    def pack(src, dst, first, second):
        src[:, TAPS * F:] = jnp.where(col == 0, jnp.broadcast_to(first, (F, F)), jnp.where(col == 1, jnp.broadcast_to(second, (F, F)), 0.0))
        for p in range(nf):
            for q in range(nx):
                dst[p * nx + q] = src[p * rows:(p + 1) * rows, q * width:(q + 1) * width]

    loss_part = jnp.sum(accr[0:1, :], axis=1, keepdims=True)
    pack(gt, ga, lanes(acc[2]), jnp.where(lax.broadcasted_iota(jnp.int32, (F, 1), 0) == 0, jnp.broadcast_to(loss_part, (F, 1)), 0.0))
    a1, a2, a3 = plane(4), line(5), plane(6)
    b1, b2, b3 = plane(7), line(8), plane(9)
    a1.scatter(ga, ra)
    ra[a1.me] = ga[a1.me]

    def fibre_back(q):
        def body(n, carry):
            cols = pl.ds(pl.multiple_of(n * 256, 256), 256)
            data = dz2[4 * q:4 * q + 10, :, cols].reshape(10 * F, 256)
            out = mm(wfr[...], data).reshape(4, F, 256)
            for j in range(4):
                dh = out[j].astype(BF).astype(F32)
                value = (dh * sl1[4 * q + j, :, cols]).astype(BF)
                dz1[4 * q + j, :, cols] = value
                value = value.astype(F32)
                acc[3] += value[:, :128] + value[:, 128:]
            return carry

        lax.fori_loop(0, T // 256, body, 0, unroll=4)

    fibre_back(0)
    fibre_back(1)
    gt2[...] = jnp.zeros_like(gt2)

    def time_grad(c, carry):
        gt2[...] += lax.dot_general(xcol[c], dz1[c], NT, preferred_element_type=F32)
        return carry

    lax.fori_loop(0, C, time_grad, 0, unroll=8)
    for k in range(TAPS):
        gt[:, k * F:(k + 1) * F] = gt2[k * F:(k + 1) * F, :].T
    pack(gt, gb, lanes(acc[3]), jnp.zeros((F, 1), F32))
    b1.scatter(gb, rb)
    rb[b1.me] = gb[b1.me]
    a1.arrive(ra)
    za[zi] = plain(ra)
    a2.spread(za)
    def time_back(c, carry):
        shifted(dz1[c], dcol, -1)
        for n in range(0, T, 256):
            gr_ref[c, :, n:n + 256] = mm(wtt[...], dcol[:, n:n + 256]).astype(BF)
        return carry

    lax.fori_loop(0, 4, time_back, 0, unroll=4)
    b1.arrive(rb)
    zb[zi] = plain(rb)
    b2.spread(zb)
    a2.arrive(za)
    fa[a3.me] = plain(za)
    a3.spread(fa)
    lax.fori_loop(4, C, time_back, 0, unroll=4)
    b2.arrive(zb)
    fb[b3.me] = plain(zb)
    b3.spread(fb)

    def unpack(buf, out):
        whole = jnp.concatenate(
            [jnp.concatenate([buf[p * nx + q] for q in range(nx)], axis=1) for p in range(nf)], axis=0
        )
        value = whole / cells
        for k in range(TAPS):
            out[k] = value[:, k * F:(k + 1) * F]
        return whole[:, TAPS * F:]

    a3.arrive(fa)
    tail = unpack(fa, gwf_ref)
    vec_ref[3:4, :F] = to_row(tail[:, 0:1] / cells)
    vec_ref[4:5, :F] = jnp.broadcast_to(tail[0:1, 1:2] / total, (1, F))
    b3.arrive(fb)
    tail = unpack(fb, gwt_ref)
    vec_ref[0:1, :F] = to_row(tail[:, 0:1] / cells)

    for group, buf in (
        (p1, sp1), (z1, sz1), (p2, sp2), (z2_, sz2),
        (a1, ga), (a2, za), (a3, fa), (b1, gb), (b2, zb), (b3, fb),
    ):
        group.done(buf)

    @pl.when(has_l)
    def _():
        dl_copy("l").wait_send()
        for c in range(2 * HALF):
            halo(c, "l").wait_send()

    @pl.when(has_r)
    def _():
        dl_copy("r").wait_send()
        for c in range(2 * HALF):
            halo(C - 1 - c, "r").wait_send()


def hand_out(gr, gwt, gwf, vec, gr_ref, gwt_ref, gbt_ref, gwf_ref, gga_ref, gbe_ref, gwh_ref, loss_ref, held, sem):
    n = held.shape[0]
    fetch = [pltpu.make_async_copy(gr.at[i], held.at[i], sem.at[i]) for i in range(n)]
    store = [pltpu.make_async_copy(held.at[i], gr_ref.at[i], sem.at[n + i]) for i in range(n)]
    store.append(pltpu.make_async_copy(gwt, gwt_ref, sem.at[2 * n]))
    store.append(pltpu.make_async_copy(gwf, gwf_ref, sem.at[2 * n + 1]))
    for copy in fetch:
        copy.start()
    for copy in store[n:]:
        copy.start()
    for i, ref in enumerate((gbt_ref, gga_ref, gbe_ref, gwh_ref)):
        ref[...] = vec[i:i + 1, :F]
    loss_ref[...] = vec[4:5, 0:1]
    for a, b in zip(fetch, store):
        a.wait()
        b.start()
    for copy in store:
        copy.wait()


def local(dims, records, labels, w_time, b_time, w_fibre, gamma, beta, w_head, b_head):
    nf, nx, nz, C, T = dims
    vm = pl.BlockSpec(memory_space=pltpu.VMEM)
    anywhere = pl.BlockSpec(memory_space=pl.ANY)
    S = jax.ShapeDtypeStruct
    V = pltpu.VMEM
    D = pltpu.SemaphoreType.DMA
    n = nf * nx
    rows, width = F // nf, 512 // nx

    def large():
        return [V((n, rows, width), F32), V((n, rows, width), F32), V((nz, rows, width), F32), V((n, rows, width), F32)]

    gr, gwt, gwf, vec = pl.pallas_call(
        functools.partial(kernel, dims),
        out_shape=(S((C, F, T), BF), S((TAPS, F, F), F32), S((TAPS, F, F), F32), S((8, 128), F32)),
        in_specs=[vm] * 8 + [pl.BlockSpec(memory_space=pltpu.SMEM)],
        out_specs=[vm] * 4,
        scratch_shapes=[
            V((F, TAPS * F), BF), V((F, TAPS * F), BF), V((4 * F, 10 * F), BF), V((4 * F, 10 * F), BF),
            V((C, TAPS * F, T), BF), V((TAPS * F, T), BF), V((C + 12, F, T), BF), V((C, F, T), F32),
            V((C + 6, F, T), F32), V((C + 6, F, T), F32), V((C + 6, F, T), BF), V((C, F, T), BF),
            V((8, F, 128), F32), V((4, F, 128), F32), V((8, 128), F32),
            V((C, 1, T), F32), V((C, 1, T), F32), V((HALF, 1, T), F32), V((HALF, 1, T), F32),
            V((F, 512), F32), V((TAPS * F, F), F32),
            V((n, 1, 128), F32), V((nz, 1, 128), F32), V((n, 1, 128), F32), V((nz, 1, 128), F32),
            *large(), *large(),
            D((12,)), D((12,)), D((2,)), D((2,)), D((20,)),
        ],
        compiler_params=pltpu.CompilerParams(
            collective_id=0, has_side_effects=True, vmem_limit_bytes=56 * 1024 * 1024
        ),
    )(
        records[0], labels[0], w_time, b_time.reshape(1, F), w_fibre, gamma.reshape(1, F), beta.reshape(1, F),
        w_head.reshape(1, F), b_head.reshape(1, 1),
    )
    row = S((1, F), F32)
    gr, gwt, gbt, gwf, gga, gbe, gwh, loss = pl.pallas_call(
        hand_out,
        out_shape=(S((C, F, T), BF), S((TAPS, F, F), F32), row, S((TAPS, F, F), F32), row, row, row, S((1, 1), F32)),
        in_specs=[anywhere] + [vm] * 3,
        out_specs=[anywhere, anywhere, vm, anywhere] + [vm] * 4,
        scratch_shapes=[V((C, F, T), BF), D((2 * C + 2,))],
        compiler_params=pltpu.CompilerParams(vmem_limit_bytes=60 * 1024 * 1024),
    )(gr, gwt, gwf, vec)
    return gr[None], gwt, gbt[0], gwf, gga[0], gbe[0], gwh[0], loss[0, 0]


def solution(mesh):
    nf, nr = mesh.shape["fibre"], mesh.shape["record"]
    nx = 4 if nr % 4 == 0 else 1

    def run(records, *rest):
        dims = (nf, nx, nr // nx, records.shape[1] // nf, records.shape[3])
        return jax.shard_map(
            functools.partial(local, dims),
            mesh=mesh,
            in_specs=(P("record", "fibre", None, None), P("record", "fibre", None)) + (P(),) * 7,
            out_specs=(P("record", "fibre", None, None),) + (P(),) * 7,
            check_vma=False,
        )(records, *rest)

    return run
```

```python
import functools

import jax
import jax.numpy as jnp
from jax import lax
from jax.experimental import pallas as pl
from jax.experimental.pallas import tpu as pltpu
from jax.sharding import PartitionSpec as P

F = 64
TAPS = 7
DILATION = 2
HALF = 3
EPS = 1e-05
BF = jnp.bfloat16
F32 = jnp.float32
MESH = pl.DeviceIdType.MESH
NT = (((1,), (1,)), ((), ()))


def mm(a, b):
    return jnp.dot(a, b, preferred_element_type=F32)


def sigmoid(v):
    return 0.5 * jnp.tanh(0.5 * v) + 0.5


def eye():
    return lax.broadcasted_iota(jnp.int32, (F, F), 0) == lax.broadcasted_iota(jnp.int32, (F, F), 1)


def to_col(row):
    return jnp.sum(jnp.where(eye(), jnp.broadcast_to(row, (F, F)), 0.0), axis=1, keepdims=True)


def to_row(col):
    return jnp.sum(jnp.where(eye(), jnp.broadcast_to(col, (F, F)), 0.0), axis=0, keepdims=True)


def wide(row):
    return jnp.broadcast_to(to_col(row), (F, 128))


class Group:
    def __init__(self, n, me, target, send, recv):
        self.n, self.me, self.target, self.send, self.recv = n, me, target, send, recv

    def peers(self):
        return [lax.rem(self.me + d, self.n) for d in range(1, self.n)]

    def copy(self, src, dst, p):
        return pltpu.make_async_remote_copy(
            src_ref=src, dst_ref=dst, send_sem=self.send, recv_sem=self.recv,
            device_id=self.target(p), device_id_type=MESH,
        )

    def spread(self, buf):
        for p in self.peers():
            self.copy(buf.at[self.me], buf.at[self.me], p).start()

    def scatter(self, src, buf):
        for p in self.peers():
            self.copy(src.at[p], buf.at[self.me], p).start()

    def all_bytes(self, buf):
        rest = buf.at[pl.ds(0, self.n - 1)]
        return self.copy(rest, rest, self.me)

    def arrive(self, buf):
        if self.n > 1:
            self.all_bytes(buf).wait_recv()

    def done(self, buf):
        if self.n > 1:
            self.all_bytes(buf).wait_send()


def kernel(
    dims,
    x_ref, lab_ref, wt_ref, bt_ref, wf_ref, gam_ref, bet_ref, wh_ref, bh_ref,
    gr_ref, gwt_ref, gwf_ref, vec_ref,
    wts, wtt, wfb, wfr, xcol, dcol, h1, sl1, z2, sl2, dz2, dz1, par, acc, accr, lab, dl, dll, dlr,
    gt, gt2,
    sp1, sz1, sp2, sz2,
    ga, ra, za, fa, gb, rb, zb, fb,
    hs, hr, ds, dr, sem, xs, gs, io,
):
    nf, nx, nz, C, T = dims
    total = float(nf * nx * nz * C * T)
    cells = float(nf * C * T)
    fi = lax.axis_index("fibre")
    ri = lax.axis_index("record")
    xi, zi = ri // nz, lax.rem(ri, nz)

    def plane(i):
        return Group(
            nf * nx, fi * nx + xi, lambda p: (p // nx, lax.rem(p, nx) * nz + zi), sem.at[2 * i], sem.at[2 * i + 1]
        )

    def line(i):
        return Group(nz, zi, lambda p: (fi, xi * nz + p), sem.at[2 * i], sem.at[2 * i + 1])

    def fetch(c):
        return pltpu.make_async_copy(x_ref.at[c], xs.at[c], io.at[c])

    def store(c):
        return pltpu.make_async_copy(gs.at[c], gr_ref.at[c], io.at[C + c])

    for i in range(C):
        fetch(i // 2 if i % 2 == 0 else C - 1 - i // 2).start()

    barrier = pltpu.get_barrier_semaphore()
    for group in (plane(0), line(1)):
        for p in group.peers():
            pl.semaphore_signal(barrier, inc=1, device_id=group.target(p), device_id_type=MESH)

    for k in range(TAPS):
        wts[:, k * F:(k + 1) * F] = wt_ref[k]
        wtt[:, k * F:(k + 1) * F] = wt_ref[k].astype(F32).T.astype(BF)
    wfb[...] = jnp.zeros_like(wfb)
    wfr[...] = jnp.zeros_like(wfr)
    for k in range(TAPS):
        w = wf_ref[k]
        wr = wf_ref[TAPS - 1 - k].astype(F32).T.astype(BF)
        for j in range(4):
            wfb[j * F:(j + 1) * F, (j + k) * F:(j + k + 1) * F] = w
            wfr[j * F:(j + 1) * F, (j + k) * F:(j + k + 1) * F] = wr
    for c in range(C):
        lab[c] = lab_ref[c:c + 1, :].astype(F32)
    par[0] = wide(bt_ref[...])
    acc[...] = jnp.zeros_like(acc)
    accr[...] = jnp.zeros_like(accr)

    has_l, has_r = fi > 0, fi < nf - 1
    left, right = lax.rem(fi + nf - 1, nf), lax.rem(fi + 1, nf)

    @pl.when(jnp.logical_not(has_l))
    def _():
        for i in range(2 * HALF):
            h1[i] = jnp.zeros((F, T), BF)
        for i in range(HALF):
            dz2[i] = jnp.zeros((F, T), BF)

    @pl.when(jnp.logical_not(has_r))
    def _():
        for i in range(2 * HALF):
            h1[2 * HALF + C + i] = jnp.zeros((F, T), BF)
        for i in range(HALF):
            dz2[HALF + C + i] = jnp.zeros((F, T), BF)

    def halo(c, side):
        slot = c + 2 * HALF + C if side == "l" else c + 2 * HALF - C
        index = c + 2 * HALF if side == "l" else c + 2 * HALF - C
        return pltpu.make_async_remote_copy(
            src_ref=h1.at[c + 2 * HALF],
            dst_ref=h1.at[slot],
            send_sem=hs.at[index],
            recv_sem=hr.at[index],
            device_id=(left if side == "l" else right, ri),
            device_id_type=MESH,
        )

    def halo_arrive(i, side):
        slot = i if side == "l" else i + 2 * HALF + C
        index = i if side == "l" else i + 2 * HALF
        pltpu.make_async_remote_copy(
            src_ref=h1.at[slot], dst_ref=h1.at[slot], send_sem=hs.at[index], recv_sem=hr.at[index],
            device_id=(left if side == "l" else right, ri), device_id_type=MESH,
        ).wait_recv()

    lane = lax.broadcasted_iota(jnp.int32, (F, 128), 1)

    def shifted(src, dst, sign):
        for k in range(TAPS):
            s = sign * DILATION * (k - HALF)
            rows = slice(k * F, (k + 1) * F)
            if s == 0:
                dst[rows, :] = src.astype(BF)
                continue
            r = pltpu.roll(src, (-s) % T, 1)
            dst[rows, :] = r.astype(BF)
            if s > 0:
                dst[rows, T - 128:] = jnp.where(lane < 128 - s, r[:, T - 128:], jnp.zeros((), r.dtype)).astype(BF)
            else:
                dst[rows, :128] = jnp.where(lane >= -s, r[:, :128], jnp.zeros((), r.dtype)).astype(BF)

    def forward(i, carry):
        c = jnp.where(lax.rem(i, 2) == 0, i // 2, C - 1 - i // 2)
        fetch(c).wait()
        shifted(xs[c], xcol.at[c], 1)
        for n in range(0, T, 256):
            pre2 = mm(wts[...], xcol[c, :, n:n + 256])
            for m in range(0, 256, 128):
                cols = slice(n + m, n + m + 128)
                pre = pre2[:, m:m + 128] + par[0]
                s = sigmoid(pre)
                h = pre * s
                h1[c + 2 * HALF, :, cols] = h.astype(BF)
                sl1[c, :, cols] = s + h * (1.0 - s)

        return carry

    def forward_send(i, carry):
        c = jnp.where(lax.rem(i, 2) == 0, i // 2, C - 1 - i // 2)
        forward(i, carry)

        @pl.when(jnp.logical_and(has_l, c < HALF))
        def _():
            halo(c, "l").start()

        @pl.when(jnp.logical_and(has_r, c >= C - HALF))
        def _():
            halo(c, "r").start()

        return carry

    lax.fori_loop(0, 2, forward, 0, unroll=2)
    pl.semaphore_wait(barrier, nf * nx + nz - 2)

    @pl.when(has_l)
    def _():
        halo(0, "l").start()

    @pl.when(has_r)
    def _():
        halo(C - 1, "r").start()

    lax.fori_loop(2, C, forward_send, 0, unroll=6)
    for d in range(HALF):
        @pl.when(has_l)
        def _():
            halo(HALF + d, "l").start()

        @pl.when(has_r)
        def _():
            halo(C - HALF - 1 - d, "r").start()

    def fibre_conv(first, count, lo):
        def body(n, carry):
            cols = pl.ds(pl.multiple_of(n * 256, 256), 256)
            data = h1[lo:lo + count + 2 * HALF, :, cols].reshape((count + 2 * HALF) * F, 256)
            out = mm(wfb[:count * F, :(count + 2 * HALF) * F], data)
            z2[first:first + count, :, cols] = out.reshape(count, F, 256)
            return carry

        lax.fori_loop(0, T // 256, body, 0, unroll=4)

    @pl.when(has_l)
    def _():
        for i in range(HALF):
            halo_arrive(HALF + i, "l")

    fibre_conv(HALF, 4, HALF)

    @pl.when(has_r)
    def _():
        for i in range(HALF):
            halo_arrive(i, "r")

    fibre_conv(HALF + 4, 4, HALF + 4)

    def add_up(c, total_):
        for n in range(0, T, 128):
            total_ = total_ + z2[HALF + c, :, n:n + 128]
        return total_

    zero = jnp.zeros((F, 128), F32)
    own_mean = jnp.sum(lax.fori_loop(0, C, add_up, zero), axis=1, keepdims=True) / float(C * T)
    own_wide = jnp.broadcast_to(own_mean, (F, 128))

    def spread_up(c, total_):
        for n in range(0, T, 128):
            d = z2[HALF + c, :, n:n + 128] - own_wide
            total_ = total_ + d * d
        return total_

    own_m2 = jnp.sum(lax.fori_loop(0, C, spread_up, zero), axis=1, keepdims=True)

    def merge(buf, n, count):
        value = buf[...]
        total_ = jnp.sum(value, axis=0)
        d = value - total_[None] * (1.0 / n)
        m2 = jnp.sum(d * d, axis=0) * count
        return jnp.concatenate([total_[:, :F] * (1.0 / n), total_[:, F:] + m2[:, :F]], axis=1)

    def plain(buf):
        return jnp.sum(buf[...], axis=0)

    p1, z1 = plane(0), line(1)
    sp1[p1.me] = jnp.concatenate([to_row(own_mean), to_row(own_m2)], axis=1)
    p1.spread(sp1)

    p1.arrive(sp1)
    sz1[zi] = merge(sp1, nf * nx, float(C * T))
    z1.spread(sz1)

    @pl.when(has_l)
    def _():
        for i in range(HALF):
            halo_arrive(i, "l")
        fibre_conv(0, HALF, 0)

    @pl.when(has_r)
    def _():
        for i in range(HALF):
            halo_arrive(HALF + i, "r")
        fibre_conv(HALF + C, HALF, HALF + C)

    z1.arrive(sz1)
    stats = merge(sz1, nz, float(C * T * nf * nx))
    mean_row = stats[:, :F]
    rstd_row = lax.rsqrt(stats[:, F:] / total + EPS)
    par[1] = wide(mean_row)
    par[2] = wide(gam_ref[...] * rstd_row)
    par[3] = wide(bet_ref[...])
    par[4] = wide(wh_ref[...].astype(F32))
    par[5] = wide(rstd_row)

    bias = bh_ref[0, 0]

    def head(c, carry):
        for n in range(0, T, 128):
            cols = slice(n, n + 128)
            zc = z2[HALF + c, :, cols] - par[1]
            act = zc * par[2] + par[3]
            s = sigmoid(act)
            h = act * s
            h2 = h.astype(BF).astype(F32)
            logit = jnp.sum(h2 * par[4], axis=0, keepdims=True) + bias
            target = lab[c, :, cols]
            soft = jnp.maximum(logit, 0.0) + jnp.log1p(jnp.exp(-jnp.abs(logit)))
            accr[0:1, :] += soft - target * logit
            dlogit = sigmoid(logit) - target
            dl[c, :, cols] = dlogit
            dh2 = (dlogit * par[4]).astype(BF).astype(F32)
            dact = dh2 * (s + h * (1.0 - s))
            sl2[HALF + c, :, cols] = dact
            acc[0] += dact
            acc[1] += dact * zc
            acc[2] += dlogit * h2
        return carry

    lax.fori_loop(0, C, head, 0, unroll=4)

    def dl_copy(side):
        i = 0 if side == "l" else 1
        return pltpu.make_async_remote_copy(
            src_ref=dl.at[0:HALF] if side == "l" else dl.at[C - HALF:C], dst_ref=dlr if side == "l" else dll, send_sem=ds.at[i], recv_sem=dr.at[i],
            device_id=(left if side == "l" else right, ri), device_id_type=MESH,
        )

    def dl_arrive(side):
        i = 1 if side == "l" else 0
        buf = dll if side == "l" else dlr
        pltpu.make_async_remote_copy(
            src_ref=buf, dst_ref=buf, send_sem=ds.at[i], recv_sem=dr.at[i],
            device_id=(left if side == "l" else right, ri), device_id_type=MESH,
        ).wait_recv()

    @pl.when(has_l)
    def _():
        dl_copy("l").start()

    @pl.when(has_r)
    def _():
        dl_copy("r").start()

    def lanes(v):
        return jnp.sum(v, axis=1, keepdims=True)

    p2, z2_ = plane(2), line(3)
    sp2[p2.me] = jnp.concatenate([to_row(lanes(acc[0])), to_row(lanes(acc[1]))], axis=1)
    p2.spread(sp2)

    def halo_dact(slot, buf, row):
        for n in range(0, T, 128):
            cols = slice(n, n + 128)
            act = (z2[slot, :, cols] - par[1]) * par[2] + par[3]
            s = sigmoid(act)
            dh2 = (buf[row, :, cols] * par[4]).astype(BF).astype(F32)
            sl2[slot, :, cols] = dh2 * (s + act * s * (1.0 - s))

    def halo_left(i, carry):
        halo_dact(i, dll, i)
        return carry

    def halo_right(i, carry):
        halo_dact(HALF + C + i, dlr, i)
        return carry

    @pl.when(has_l)
    def _():
        dl_arrive("l")
        lax.fori_loop(0, HALF, halo_left, 0)

    p2.arrive(sp2)
    sz2[zi] = plain(sp2)
    z2_.spread(sz2)

    @pl.when(has_r)
    def _():
        dl_arrive("r")
        lax.fori_loop(0, HALF, halo_right, 0)

    z2_.arrive(sz2)
    sums = plain(sz2)
    rstd_row = to_row(par[5][:, 0:1])
    beta_row = sums[:, :F]
    gamma_row = sums[:, F:] * rstd_row
    vec_ref[2:3, :F] = beta_row / cells
    vec_ref[1:2, :F] = gamma_row / cells
    par[6] = wide(beta_row / total)
    par[7] = wide(gamma_row * rstd_row / total)

    def slope_back(slot, carry):
        for n in range(0, T, 128):
            cols = slice(n, n + 128)
            zc = z2[slot, :, cols] - par[1]
            dz2[slot, :, cols] = (par[2] * (sl2[slot, :, cols] - par[6] - zc * par[7])).astype(BF)
        return carry

    lax.fori_loop(HALF, HALF + C, slope_back, 0, unroll=2)

    @pl.when(has_l)
    def _():
        lax.fori_loop(0, HALF, slope_back, 0)

    @pl.when(has_r)
    def _():
        lax.fori_loop(C + HALF, C + 2 * HALF, slope_back, 0)


    for q in range(2):
        grad = lax.dot_general(
            dz2[HALF + 4 * q:HALF + 4 * q + 4].reshape(4 * F, T),
            h1[HALF + 4 * q:HALF + 4 * q + 10].reshape(10 * F, T),
            NT, preferred_element_type=F32,
        )
        for j in range(4):
            piece = grad[j * F:(j + 1) * F, j * F:(j + TAPS) * F]
            if q == 0 and j == 0:
                gt[:, :TAPS * F] = piece
            else:
                gt[:, :TAPS * F] += piece
    col = lax.broadcasted_iota(jnp.int32, (F, F), 1)

    rows, width = F // nf, 512 // nx

    def pack(src, dst, first, second):
        src[:, TAPS * F:] = jnp.where(col == 0, jnp.broadcast_to(first, (F, F)), jnp.where(col == 1, jnp.broadcast_to(second, (F, F)), 0.0))
        for p in range(nf):
            for q in range(nx):
                dst[p * nx + q] = src[p * rows:(p + 1) * rows, q * width:(q + 1) * width]

    loss_part = jnp.sum(accr[0:1, :], axis=1, keepdims=True)
    pack(gt, ga, lanes(acc[2]), jnp.where(lax.broadcasted_iota(jnp.int32, (F, 1), 0) == 0, jnp.broadcast_to(loss_part, (F, 1)), 0.0))
    a1, a2, a3 = plane(4), line(5), plane(6)
    b1, b2, b3 = plane(7), line(8), plane(9)
    a1.scatter(ga, ra)
    ra[a1.me] = ga[a1.me]

    def fibre_back(q):
        def body(n, carry):
            cols = pl.ds(pl.multiple_of(n * 256, 256), 256)
            data = dz2[4 * q:4 * q + 10, :, cols].reshape(10 * F, 256)
            out = mm(wfr[...], data).reshape(4, F, 256)
            for j in range(4):
                dh = out[j].astype(BF).astype(F32)
                value = (dh * sl1[4 * q + j, :, cols]).astype(BF)
                dz1[4 * q + j, :, cols] = value
                value = value.astype(F32)
                acc[3] += value[:, :128] + value[:, 128:]
            return carry

        lax.fori_loop(0, T // 256, body, 0, unroll=4)

    fibre_back(0)
    fibre_back(1)
    gt2[...] = jnp.zeros_like(gt2)

    def time_grad(c, carry):
        gt2[...] += lax.dot_general(xcol[c], dz1[c], NT, preferred_element_type=F32)
        return carry

    lax.fori_loop(0, C, time_grad, 0, unroll=8)
    for k in range(TAPS):
        gt[:, k * F:(k + 1) * F] = gt2[k * F:(k + 1) * F, :].T
    pack(gt, gb, lanes(acc[3]), jnp.zeros((F, 1), F32))
    b1.scatter(gb, rb)
    rb[b1.me] = gb[b1.me]
    a1.arrive(ra)
    za[zi] = plain(ra)
    a2.spread(za)
    def time_back(c, carry):
        shifted(dz1[c], dcol, -1)
        for n in range(0, T, 256):
            gs[c, :, n:n + 256] = mm(wtt[...], dcol[:, n:n + 256]).astype(BF)
        store(c).start()
        return carry

    lax.fori_loop(0, 4, time_back, 0, unroll=4)
    b1.arrive(rb)
    zb[zi] = plain(rb)
    b2.spread(zb)
    a2.arrive(za)
    fa[a3.me] = plain(za)
    a3.spread(fa)
    lax.fori_loop(4, C, time_back, 0, unroll=4)
    b2.arrive(zb)
    fb[b3.me] = plain(zb)
    b3.spread(fb)

    def unpack(buf, out):
        whole = jnp.concatenate(
            [jnp.concatenate([buf[p * nx + q] for q in range(nx)], axis=1) for p in range(nf)], axis=0
        )
        value = whole / cells
        for k in range(TAPS):
            out[k] = value[:, k * F:(k + 1) * F]
        return whole[:, TAPS * F:]

    a3.arrive(fa)
    tail = unpack(fa, gwf_ref)
    vec_ref[3:4, :F] = to_row(tail[:, 0:1] / cells)
    vec_ref[4:5, :F] = jnp.broadcast_to(tail[0:1, 1:2] / total, (1, F))
    b3.arrive(fb)
    tail = unpack(fb, gwt_ref)
    vec_ref[0:1, :F] = to_row(tail[:, 0:1] / cells)

    for c in range(C):
        store(c).wait()
    for group, buf in (
        (p1, sp1), (z1, sz1), (p2, sp2), (z2_, sz2),
        (a1, ga), (a2, za), (a3, fa), (b1, gb), (b2, zb), (b3, fb),
    ):
        group.done(buf)

    @pl.when(has_l)
    def _():
        dl_copy("l").wait_send()
        for c in range(2 * HALF):
            halo(c, "l").wait_send()

    @pl.when(has_r)
    def _():
        dl_copy("r").wait_send()
        for c in range(2 * HALF):
            halo(C - 1 - c, "r").wait_send()


def hand_out(gr, gwt, gwf, vec, gr_ref, gwt_ref, gbt_ref, gwf_ref, gga_ref, gbe_ref, gwh_ref, loss_ref, sem):
    copies = [
        pltpu.make_async_copy(a, b, sem.at[i])
        for i, (a, b) in enumerate(((gr, gr_ref), (gwt, gwt_ref), (gwf, gwf_ref)))
    ]
    for copy in copies:
        copy.start()
    for i, ref in enumerate((gbt_ref, gga_ref, gbe_ref, gwh_ref)):
        ref[...] = vec[i:i + 1, :F]
    loss_ref[...] = vec[4:5, 0:1]
    for copy in copies:
        copy.wait()


def local(dims, records, labels, w_time, b_time, w_fibre, gamma, beta, w_head, b_head):
    nf, nx, nz, C, T = dims
    vm = pl.BlockSpec(memory_space=pltpu.VMEM)
    anywhere = pl.BlockSpec(memory_space=pl.ANY)
    S = jax.ShapeDtypeStruct
    V = pltpu.VMEM
    D = pltpu.SemaphoreType.DMA
    n = nf * nx
    rows, width = F // nf, 512 // nx

    def large():
        return [V((n, rows, width), F32), V((n, rows, width), F32), V((nz, rows, width), F32), V((n, rows, width), F32)]

    gr, gwt, gwf, vec = pl.pallas_call(
        functools.partial(kernel, dims),
        out_shape=(S((C, F, T), BF), S((TAPS, F, F), F32), S((TAPS, F, F), F32), S((8, 128), F32)),
        in_specs=[anywhere] + [vm] * 7 + [pl.BlockSpec(memory_space=pltpu.SMEM)],
        out_specs=[anywhere] + [vm] * 3,
        scratch_shapes=[
            V((F, TAPS * F), BF), V((F, TAPS * F), BF), V((4 * F, 10 * F), BF), V((4 * F, 10 * F), BF),
            V((C, TAPS * F, T), BF), V((TAPS * F, T), BF), V((C + 12, F, T), BF), V((C, F, T), F32),
            V((C + 6, F, T), F32), V((C + 6, F, T), F32), V((C + 6, F, T), BF), V((C, F, T), BF),
            V((8, F, 128), F32), V((4, F, 128), F32), V((8, 128), F32),
            V((C, 1, T), F32), V((C, 1, T), F32), V((HALF, 1, T), F32), V((HALF, 1, T), F32),
            V((F, 512), F32), V((TAPS * F, F), F32),
            V((n, 1, 128), F32), V((nz, 1, 128), F32), V((n, 1, 128), F32), V((nz, 1, 128), F32),
            *large(), *large(),
            D((12,)), D((12,)), D((2,)), D((2,)), D((20,)),
            V((C, F, T), BF), V((C, F, T), BF), D((2 * C,)),
        ],
        compiler_params=pltpu.CompilerParams(
            collective_id=0, has_side_effects=True, vmem_limit_bytes=60 * 1024 * 1024
        ),
    )(
        records[0], labels[0], w_time, b_time.reshape(1, F), w_fibre, gamma.reshape(1, F), beta.reshape(1, F),
        w_head.reshape(1, F), b_head.reshape(1, 1),
    )
    row = S((1, F), F32)
    gr, gwt, gbt, gwf, gga, gbe, gwh, loss = pl.pallas_call(
        hand_out,
        out_shape=(S((C, F, T), BF), S((TAPS, F, F), F32), row, S((TAPS, F, F), F32), row, row, row, S((1, 1), F32)),
        in_specs=[vm] * 4,
        out_specs=[anywhere, anywhere, vm, anywhere] + [vm] * 4,
        scratch_shapes=[D((3,))],
        compiler_params=pltpu.CompilerParams(vmem_limit_bytes=60 * 1024 * 1024),
    )(gr, gwt, gwf, vec)
    return gr[None], gwt, gbt[0], gwf, gga[0], gbe[0], gwh[0], loss[0, 0]


def solution(mesh):
    nf, nr = mesh.shape["fibre"], mesh.shape["record"]
    nx = 4 if nr % 4 == 0 else 1

    def run(records, *rest):
        dims = (nf, nx, nr // nx, records.shape[1] // nf, records.shape[3])
        return jax.shard_map(
            functools.partial(local, dims),
            mesh=mesh,
            in_specs=(P("record", "fibre", None, None), P("record", "fibre", None)) + (P(),) * 7,
            out_specs=(P("record", "fibre", None, None),) + (P(),) * 7,
            check_vma=False,
        )(records, *rest)

    return run
```

```python
import functools

import jax
import jax.numpy as jnp
from jax import lax
from jax.experimental import pallas as pl
from jax.experimental.pallas import tpu as pltpu
from jax.sharding import PartitionSpec as P

F = 64
TAPS = 7
DILATION = 2
HALF = 3
EPS = 1e-05
BF = jnp.bfloat16
F32 = jnp.float32
MESH = pl.DeviceIdType.MESH
NT = (((1,), (1,)), ((), ()))


def mm(a, b):
    return jnp.dot(a, b, preferred_element_type=F32)


def sigmoid(v):
    return 0.5 * jnp.tanh(0.5 * v) + 0.5


def eye():
    return lax.broadcasted_iota(jnp.int32, (F, F), 0) == lax.broadcasted_iota(jnp.int32, (F, F), 1)


def to_col(row):
    return jnp.sum(jnp.where(eye(), jnp.broadcast_to(row, (F, F)), 0.0), axis=1, keepdims=True)


def to_row(col):
    return jnp.sum(jnp.where(eye(), jnp.broadcast_to(col, (F, F)), 0.0), axis=0, keepdims=True)


def wide(row):
    return jnp.broadcast_to(to_col(row), (F, 128))


class Group:
    def __init__(self, n, me, target, send, recv):
        self.n, self.me, self.target, self.send, self.recv = n, me, target, send, recv

    def peers(self):
        return [lax.rem(self.me + d, self.n) for d in range(1, self.n)]

    def copy(self, src, dst, p):
        return pltpu.make_async_remote_copy(
            src_ref=src, dst_ref=dst, send_sem=self.send, recv_sem=self.recv,
            device_id=self.target(p), device_id_type=MESH,
        )

    def spread(self, buf):
        for p in self.peers():
            self.copy(buf.at[self.me], buf.at[self.me], p).start()

    def scatter(self, src, buf):
        for p in self.peers():
            self.copy(src.at[p], buf.at[self.me], p).start()

    def all_bytes(self, buf):
        rest = buf.at[pl.ds(0, self.n - 1)]
        return self.copy(rest, rest, self.me)

    def arrive(self, buf):
        if self.n > 1:
            self.all_bytes(buf).wait_recv()

    def done(self, buf):
        if self.n > 1:
            self.all_bytes(buf).wait_send()


def kernel(
    dims,
    x_ref, lab_ref, wt_ref, bt_ref, wf_ref, gam_ref, bet_ref, wh_ref, bh_ref,
    gr_ref, gwt_ref, gwf_ref, vec_ref,
    wts, wtt, wfb, wfr, xcol, dcol, h1, sl1, z2, sl2, dz2, dz1, par, acc, accr, lab, dl, dll, dlr,
    gt,
    sp1, sz1, sp2, sz2,
    ga, ra, za, fa, gb, rb, zb, fb,
    hs, hr, ds, dr, sem, xs, gs, io,
):
    nf, nx, nz, C, T = dims
    total = float(nf * nx * nz * C * T)
    cells = float(nf * C * T)
    fi = lax.axis_index("fibre")
    ri = lax.axis_index("record")
    xi, zi = ri // nz, lax.rem(ri, nz)

    def plane(i):
        return Group(
            nf * nx, fi * nx + xi, lambda p: (p // nx, lax.rem(p, nx) * nz + zi), sem.at[2 * i], sem.at[2 * i + 1]
        )

    def line(i):
        return Group(nz, zi, lambda p: (fi, xi * nz + p), sem.at[2 * i], sem.at[2 * i + 1])

    def fetch(c):
        return pltpu.make_async_copy(x_ref.at[c], xs.at[c], io.at[c])

    def store(c):
        return pltpu.make_async_copy(gs.at[c], gr_ref.at[c], io.at[C + c])

    for i in range(C):
        fetch(i // 2 if i % 2 == 0 else C - 1 - i // 2).start()

    barrier = pltpu.get_barrier_semaphore()
    for group in (plane(0), line(1)):
        for p in group.peers():
            pl.semaphore_signal(barrier, inc=1, device_id=group.target(p), device_id_type=MESH)

    for k in range(TAPS):
        wts[:, k * F:(k + 1) * F] = wt_ref[k]
    par[0] = wide(bt_ref[...])

    has_l, has_r = fi > 0, fi < nf - 1
    left, right = lax.rem(fi + nf - 1, nf), lax.rem(fi + 1, nf)

    @pl.when(jnp.logical_not(has_l))
    def _():
        for i in range(2 * HALF):
            h1[i] = jnp.zeros((F, T), BF)
        for i in range(HALF):
            dz2[i] = jnp.zeros((F, T), BF)

    @pl.when(jnp.logical_not(has_r))
    def _():
        for i in range(2 * HALF):
            h1[2 * HALF + C + i] = jnp.zeros((F, T), BF)
        for i in range(HALF):
            dz2[HALF + C + i] = jnp.zeros((F, T), BF)

    def halo(c, side):
        slot = c + 2 * HALF + C if side == "l" else c + 2 * HALF - C
        index = c + 2 * HALF if side == "l" else c + 2 * HALF - C
        return pltpu.make_async_remote_copy(
            src_ref=h1.at[c + 2 * HALF],
            dst_ref=h1.at[slot],
            send_sem=hs.at[index],
            recv_sem=hr.at[index],
            device_id=(left if side == "l" else right, ri),
            device_id_type=MESH,
        )

    def halo_arrive(i, side):
        slot = i if side == "l" else i + 2 * HALF + C
        index = i if side == "l" else i + 2 * HALF
        pltpu.make_async_remote_copy(
            src_ref=h1.at[slot], dst_ref=h1.at[slot], send_sem=hs.at[index], recv_sem=hr.at[index],
            device_id=(left if side == "l" else right, ri), device_id_type=MESH,
        ).wait_recv()

    lane = lax.broadcasted_iota(jnp.int32, (F, 128), 1)

    def shifted(src, dst, sign):
        for k in range(TAPS):
            s = sign * DILATION * (k - HALF)
            rows = slice(k * F, (k + 1) * F)
            if s == 0:
                dst[rows, :] = src.astype(BF)
                continue
            r = pltpu.roll(src, (-s) % T, 1)
            dst[rows, :] = r.astype(BF)
            if s > 0:
                dst[rows, T - 128:] = jnp.where(lane < 128 - s, r[:, T - 128:], jnp.zeros((), r.dtype)).astype(BF)
            else:
                dst[rows, :128] = jnp.where(lane >= -s, r[:, :128], jnp.zeros((), r.dtype)).astype(BF)

    def forward(i, carry):
        c = jnp.where(lax.rem(i, 2) == 0, i // 2, C - 1 - i // 2)
        fetch(c).wait()
        shifted(xs[c], xcol.at[c], 1)
        for n in range(0, T, 256):
            pre2 = mm(wts[...], xcol[c, :, n:n + 256])
            for m in range(0, 256, 128):
                cols = slice(n + m, n + m + 128)
                pre = pre2[:, m:m + 128] + par[0]
                s = sigmoid(pre)
                h = pre * s
                h1[c + 2 * HALF, :, cols] = h.astype(BF)
                sl1[c, :, cols] = s + h * (1.0 - s)

        return carry

    def forward_send(i, carry):
        c = jnp.where(lax.rem(i, 2) == 0, i // 2, C - 1 - i // 2)
        forward(i, carry)

        @pl.when(jnp.logical_and(has_l, c < HALF))
        def _():
            halo(c, "l").start()

        @pl.when(jnp.logical_and(has_r, c >= C - HALF))
        def _():
            halo(c, "r").start()

        return carry

    lax.fori_loop(0, 2, forward, 0, unroll=2)
    pl.semaphore_wait(barrier, nf * nx + nz - 2)

    @pl.when(has_l)
    def _():
        halo(0, "l").start()

    @pl.when(has_r)
    def _():
        halo(C - 1, "r").start()

    lax.fori_loop(2, C, forward_send, 0, unroll=6)
    for d in range(HALF):
        @pl.when(has_l)
        def _():
            halo(HALF + d, "l").start()

        @pl.when(has_r)
        def _():
            halo(C - HALF - 1 - d, "r").start()

    for k in range(TAPS):
        wtt[:, k * F:(k + 1) * F] = wt_ref[k].astype(F32).T.astype(BF)
    wfb[...] = jnp.zeros_like(wfb)
    wfr[...] = jnp.zeros_like(wfr)
    for k in range(TAPS):
        w = wf_ref[k]
        wr = wf_ref[TAPS - 1 - k].astype(F32).T.astype(BF)
        for j in range(4):
            wfb[j * F:(j + 1) * F, (j + k) * F:(j + k + 1) * F] = w
            wfr[j * F:(j + 1) * F, (j + k) * F:(j + k + 1) * F] = wr
    for c in range(C):
        lab[c] = lab_ref[c:c + 1, :].astype(F32)
    par[3] = wide(bet_ref[...])
    par[4] = wide(wh_ref[...].astype(F32))
    acc[...] = jnp.zeros_like(acc)
    accr[...] = jnp.zeros_like(accr)

    def fibre_conv(first, count, lo):
        def body(n, carry):
            cols = pl.ds(pl.multiple_of(n * 256, 256), 256)
            data = h1[lo:lo + count + 2 * HALF, :, cols].reshape((count + 2 * HALF) * F, 256)
            out = mm(wfb[:count * F, :(count + 2 * HALF) * F], data)
            z2[first:first + count, :, cols] = out.reshape(count, F, 256)
            return carry

        lax.fori_loop(0, T // 256, body, 0, unroll=4)

    @pl.when(has_l)
    def _():
        for i in range(HALF):
            halo_arrive(HALF + i, "l")

    fibre_conv(HALF, 4, HALF)

    @pl.when(has_r)
    def _():
        for i in range(HALF):
            halo_arrive(i, "r")

    fibre_conv(HALF + 4, 4, HALF + 4)

    def add_up(c, total_):
        for n in range(0, T, 128):
            total_ = total_ + z2[HALF + c, :, n:n + 128]
        return total_

    zero = jnp.zeros((F, 128), F32)
    own_mean = jnp.sum(lax.fori_loop(0, C, add_up, zero, unroll=8), axis=1, keepdims=True) / float(C * T)
    own_wide = jnp.broadcast_to(own_mean, (F, 128))

    def spread_up(c, total_):
        for n in range(0, T, 128):
            d = z2[HALF + c, :, n:n + 128] - own_wide
            total_ = total_ + d * d
        return total_

    own_m2 = jnp.sum(lax.fori_loop(0, C, spread_up, zero, unroll=8), axis=1, keepdims=True)

    def merge(buf, n, count):
        value = buf[...]
        total_ = jnp.sum(value, axis=0)
        d = value - total_[None] * (1.0 / n)
        m2 = jnp.sum(d * d, axis=0) * count
        return jnp.concatenate([total_[:, :F] * (1.0 / n), total_[:, F:] + m2[:, :F]], axis=1)

    def plain(buf):
        return jnp.sum(buf[...], axis=0)

    p1, z1 = plane(0), line(1)
    sp1[p1.me] = jnp.concatenate([to_row(own_mean), to_row(own_m2)], axis=1)
    p1.spread(sp1)

    p1.arrive(sp1)
    sz1[zi] = merge(sp1, nf * nx, float(C * T))
    z1.spread(sz1)

    @pl.when(has_l)
    def _():
        for i in range(HALF):
            halo_arrive(i, "l")
        fibre_conv(0, HALF, 0)

    @pl.when(has_r)
    def _():
        for i in range(HALF):
            halo_arrive(HALF + i, "r")
        fibre_conv(HALF + C, HALF, HALF + C)

    z1.arrive(sz1)
    stats = merge(sz1, nz, float(C * T * nf * nx))
    mean_row = stats[:, :F]
    rstd_row = lax.rsqrt(stats[:, F:] / total + EPS)
    par[1] = wide(mean_row)
    par[2] = wide(gam_ref[...] * rstd_row)

    bias = bh_ref[0, 0]

    def head(c, carry):
        for n in range(0, T, 128):
            cols = slice(n, n + 128)
            zc = z2[HALF + c, :, cols] - par[1]
            act = zc * par[2] + par[3]
            s = sigmoid(act)
            h = act * s
            h2 = h.astype(BF).astype(F32)
            logit = jnp.sum(h2 * par[4], axis=0, keepdims=True) + bias
            target = lab[c, :, cols]
            soft = jnp.maximum(logit, 0.0) + jnp.log1p(jnp.exp(-jnp.abs(logit)))
            accr[0:1, :] += soft - target * logit
            dlogit = sigmoid(logit) - target
            dl[c, :, cols] = dlogit
            dh2 = (dlogit * par[4]).astype(BF).astype(F32)
            dact = dh2 * (s + h * (1.0 - s))
            sl2[HALF + c, :, cols] = dact
            acc[0] += dact
            acc[1] += dact * zc
            acc[2] += dlogit * h2
        return carry

    lax.fori_loop(0, C, head, 0, unroll=4)

    def dl_copy(side):
        i = 0 if side == "l" else 1
        return pltpu.make_async_remote_copy(
            src_ref=dl.at[0:HALF] if side == "l" else dl.at[C - HALF:C], dst_ref=dlr if side == "l" else dll, send_sem=ds.at[i], recv_sem=dr.at[i],
            device_id=(left if side == "l" else right, ri), device_id_type=MESH,
        )

    def dl_arrive(side):
        i = 1 if side == "l" else 0
        buf = dll if side == "l" else dlr
        pltpu.make_async_remote_copy(
            src_ref=buf, dst_ref=buf, send_sem=ds.at[i], recv_sem=dr.at[i],
            device_id=(left if side == "l" else right, ri), device_id_type=MESH,
        ).wait_recv()

    @pl.when(has_l)
    def _():
        dl_copy("l").start()

    @pl.when(has_r)
    def _():
        dl_copy("r").start()

    def lanes(v):
        return jnp.sum(v, axis=1, keepdims=True)

    p2, z2_ = plane(2), line(3)
    sp2[p2.me] = jnp.concatenate([to_row(lanes(acc[0])), to_row(lanes(acc[1]))], axis=1)
    p2.spread(sp2)

    def halo_dact(slot, buf, row):
        for n in range(0, T, 128):
            cols = slice(n, n + 128)
            act = (z2[slot, :, cols] - par[1]) * par[2] + par[3]
            s = sigmoid(act)
            dh2 = (buf[row, :, cols] * par[4]).astype(BF).astype(F32)
            sl2[slot, :, cols] = dh2 * (s + act * s * (1.0 - s))

    def halo_left(i, carry):
        halo_dact(i, dll, i)
        return carry

    def halo_right(i, carry):
        halo_dact(HALF + C + i, dlr, i)
        return carry

    @pl.when(has_l)
    def _():
        dl_arrive("l")
        lax.fori_loop(0, HALF, halo_left, 0)

    p2.arrive(sp2)
    sz2[zi] = plain(sp2)
    z2_.spread(sz2)

    @pl.when(has_r)
    def _():
        dl_arrive("r")
        lax.fori_loop(0, HALF, halo_right, 0)

    z2_.arrive(sz2)
    sums = plain(sz2)
    beta_row = sums[:, :F]
    gamma_row = sums[:, F:] * rstd_row
    vec_ref[2:3, :F] = beta_row / cells
    vec_ref[1:2, :F] = gamma_row / cells
    par[6] = wide(beta_row / total)
    par[7] = wide(gamma_row * rstd_row / total)

    def slope_back(slot, carry):
        for n in range(0, T, 128):
            cols = slice(n, n + 128)
            zc = z2[slot, :, cols] - par[1]
            dz2[slot, :, cols] = (par[2] * (sl2[slot, :, cols] - par[6] - zc * par[7])).astype(BF)
        return carry

    lax.fori_loop(HALF, HALF + C, slope_back, 0, unroll=4)

    @pl.when(has_l)
    def _():
        lax.fori_loop(0, HALF, slope_back, 0)

    @pl.when(has_r)
    def _():
        lax.fori_loop(C + HALF, C + 2 * HALF, slope_back, 0)


    for q in range(2):
        grad = lax.dot_general(
            dz2[HALF + 4 * q:HALF + 4 * q + 4].reshape(4 * F, T),
            h1[HALF + 4 * q:HALF + 4 * q + 10].reshape(10 * F, T),
            NT, preferred_element_type=F32,
        )
        for j in range(4):
            piece = grad[j * F:(j + 1) * F, j * F:(j + TAPS) * F]
            if q == 0 and j == 0:
                gt[:, :TAPS * F] = piece
            else:
                gt[:, :TAPS * F] += piece
    col = lax.broadcasted_iota(jnp.int32, (F, F), 1)

    rows, width = F // nf, 512 // nx

    def pack(src, dst, first, second):
        src[:, TAPS * F:] = jnp.where(col == 0, jnp.broadcast_to(first, (F, F)), jnp.where(col == 1, jnp.broadcast_to(second, (F, F)), 0.0))
        for p in range(nf):
            for q in range(nx):
                dst[p * nx + q] = src[p * rows:(p + 1) * rows, q * width:(q + 1) * width]

    loss_part = jnp.sum(accr[0:1, :], axis=1, keepdims=True)
    pack(gt, ga, lanes(acc[2]), jnp.where(lax.broadcasted_iota(jnp.int32, (F, 1), 0) == 0, jnp.broadcast_to(loss_part, (F, 1)), 0.0))
    a1, a2, a3 = plane(4), line(5), plane(6)
    b1, b2, b3 = plane(7), line(8), plane(9)
    a1.scatter(ga, ra)
    ra[a1.me] = ga[a1.me]

    def fibre_back(q):
        def body(n, carry):
            cols = pl.ds(pl.multiple_of(n * 256, 256), 256)
            data = dz2[4 * q:4 * q + 10, :, cols].reshape(10 * F, 256)
            out = mm(wfr[...], data).reshape(4, F, 256)
            for j in range(4):
                dh = out[j].astype(BF).astype(F32)
                value = (dh * sl1[4 * q + j, :, cols]).astype(BF)
                dz1[4 * q + j, :, cols] = value
                value = value.astype(F32)
                acc[3] += value[:, :128] + value[:, 128:]
            return carry

        lax.fori_loop(0, T // 256, body, 0, unroll=4)

    fibre_back(0)
    fibre_back(1)
    gt[...] = jnp.zeros_like(gt)

    def time_grad(c, carry):
        gt[:, :TAPS * F] += lax.dot_general(dz1[c], xcol[c], NT, preferred_element_type=F32)
        return carry

    lax.fori_loop(0, C, time_grad, 0, unroll=8)
    pack(gt, gb, lanes(acc[3]), jnp.zeros((F, 1), F32))
    b1.scatter(gb, rb)
    rb[b1.me] = gb[b1.me]
    a1.arrive(ra)
    za[zi] = plain(ra)
    a2.spread(za)
    def time_back(c, carry):
        shifted(dz1[c], dcol, -1)
        for n in range(0, T, 256):
            gs[c, :, n:n + 256] = mm(wtt[...], dcol[:, n:n + 256]).astype(BF)
        store(c).start()
        return carry

    lax.fori_loop(0, 4, time_back, 0, unroll=4)
    b1.arrive(rb)
    zb[zi] = plain(rb)
    b2.spread(zb)
    a2.arrive(za)
    fa[a3.me] = plain(za)
    a3.spread(fa)
    lax.fori_loop(4, C, time_back, 0, unroll=4)
    b2.arrive(zb)
    fb[b3.me] = plain(zb)
    b3.spread(fb)

    def unpack(buf, out):
        whole = jnp.concatenate(
            [jnp.concatenate([buf[p * nx + q] for q in range(nx)], axis=1) for p in range(nf)], axis=0
        )
        value = whole * (1.0 / cells)
        for k in range(TAPS):
            out[k] = value[:, k * F:(k + 1) * F]
        return whole[:, TAPS * F:]

    a3.arrive(fa)
    tail = unpack(fa, gwf_ref)
    vec_ref[3:4, :F] = to_row(tail[:, 0:1] / cells)
    vec_ref[4:5, :F] = jnp.broadcast_to(tail[0:1, 1:2] / total, (1, F))
    b3.arrive(fb)
    tail = unpack(fb, gwt_ref)
    vec_ref[0:1, :F] = to_row(tail[:, 0:1] / cells)

    for c in range(C):
        store(c).wait()
    for group, buf in (
        (p1, sp1), (z1, sz1), (p2, sp2), (z2_, sz2),
        (a1, ga), (a2, za), (a3, fa), (b1, gb), (b2, zb), (b3, fb),
    ):
        group.done(buf)

    @pl.when(has_l)
    def _():
        dl_copy("l").wait_send()
        for c in range(2 * HALF):
            halo(c, "l").wait_send()

    @pl.when(has_r)
    def _():
        dl_copy("r").wait_send()
        for c in range(2 * HALF):
            halo(C - 1 - c, "r").wait_send()


def hand_out(
    gr, gwt, gwf, vec, gr_ref, gwt_ref, gbt_ref, gwf_ref, gga_ref, gbe_ref, gwh_ref, loss_ref,
    gr_s, gwt_s, gwf_s, vec_s, gbt_s, gga_s, gbe_s, gwh_s, loss_s, come, go,
):
    half = gr_s.shape[0] // 2
    first, second = pl.ds(0, half), pl.ds(half, half)
    fetch = [
        pltpu.make_async_copy(a, b, come.at[i])
        for i, (a, b) in enumerate((
            (vec, vec_s), (gr.at[first], gr_s.at[first]), (gr.at[second], gr_s.at[second]), (gwt, gwt_s), (gwf, gwf_s),
        ))
    ]
    store = [
        pltpu.make_async_copy(a, b, go.at[i])
        for i, (a, b) in enumerate((
            (gr_s.at[first], gr_ref.at[first]), (gr_s.at[second], gr_ref.at[second]), (gwt_s, gwt_ref), (gwf_s, gwf_ref),
            (gbt_s, gbt_ref), (gga_s, gga_ref), (gbe_s, gbe_ref), (gwh_s, gwh_ref), (loss_s, loss_ref),
        ))
    ]
    for copy in fetch:
        copy.start()
    fetch[0].wait()
    for i, ref in enumerate((gbt_s, gga_s, gbe_s, gwh_s)):
        ref[...] = vec_s[i:i + 1, :F]
    loss_s[...] = vec_s[4:5, 0:1]
    for copy in store[4:]:
        copy.start()
    for a, b in zip(fetch[1:], store[:4]):
        a.wait()
        b.start()
    for copy in store:
        copy.wait()


def local(dims, records, labels, w_time, b_time, w_fibre, gamma, beta, w_head, b_head):
    nf, nx, nz, C, T = dims
    vm = pl.BlockSpec(memory_space=pltpu.VMEM)
    anywhere = pl.BlockSpec(memory_space=pl.ANY)
    S = jax.ShapeDtypeStruct
    V = pltpu.VMEM
    D = pltpu.SemaphoreType.DMA
    n = nf * nx
    rows, width = F // nf, 512 // nx

    def large():
        return [V((n, rows, width), F32), V((n, rows, width), F32), V((nz, rows, width), F32), V((n, rows, width), F32)]

    gr, gwt, gwf, vec = pl.pallas_call(
        functools.partial(kernel, dims),
        out_shape=(S((C, F, T), BF), S((TAPS, F, F), F32), S((TAPS, F, F), F32), S((8, 128), F32)),
        in_specs=[anywhere] + [vm] * 7 + [pl.BlockSpec(memory_space=pltpu.SMEM)],
        out_specs=[anywhere] + [vm] * 3,
        scratch_shapes=[
            V((F, TAPS * F), BF), V((F, TAPS * F), BF), V((4 * F, 10 * F), BF), V((4 * F, 10 * F), BF),
            V((C, TAPS * F, T), BF), V((TAPS * F, T), BF), V((C + 12, F, T), BF), V((C, F, T), F32),
            V((C + 6, F, T), F32), V((C + 6, F, T), F32), V((C + 6, F, T), BF), V((C, F, T), BF),
            V((8, F, 128), F32), V((4, F, 128), F32), V((8, 128), F32),
            V((C, 1, T), F32), V((C, 1, T), F32), V((HALF, 1, T), F32), V((HALF, 1, T), F32),
            V((F, 512), F32),
            V((n, 1, 128), F32), V((nz, 1, 128), F32), V((n, 1, 128), F32), V((nz, 1, 128), F32),
            *large(), *large(),
            D((12,)), D((12,)), D((2,)), D((2,)), D((20,)),
            V((C, F, T), BF), V((C, F, T), BF), D((2 * C,)),
        ],
        compiler_params=pltpu.CompilerParams(
            collective_id=0, has_side_effects=True, vmem_limit_bytes=60 * 1024 * 1024
        ),
    )(
        records[0], labels[0], w_time, b_time.reshape(1, F), w_fibre, gamma.reshape(1, F), beta.reshape(1, F),
        w_head.reshape(1, F), b_head.reshape(1, 1),
    )
    row = S((1, F), F32)
    gr, gwt, gbt, gwf, gga, gbe, gwh, loss = pl.pallas_call(
        hand_out,
        out_shape=(S((C, F, T), BF), S((TAPS, F, F), F32), row, S((TAPS, F, F), F32), row, row, row, S((1, 1), F32)),
        in_specs=[anywhere] * 4,
        out_specs=[anywhere] * 8,
        scratch_shapes=[
            V((C, F, T), BF), V((TAPS, F, F), F32), V((TAPS, F, F), F32), V((8, 128), F32),
            V((1, F), F32), V((1, F), F32), V((1, F), F32), V((1, F), F32), V((1, 1), F32), D((5,)), D((9,)),
        ],
        compiler_params=pltpu.CompilerParams(vmem_limit_bytes=60 * 1024 * 1024),
    )(gr, gwt, gwf, vec)
    return gr[None], gwt, gbt[0], gwf, gga[0], gbe[0], gwh[0], loss[0, 0]


def solution(mesh):
    nf, nr = mesh.shape["fibre"], mesh.shape["record"]
    nx = 4 if nr % 4 == 0 else 1

    def run(records, *rest):
        dims = (nf, nx, nr // nx, records.shape[1] // nf, records.shape[3])
        return jax.shard_map(
            functools.partial(local, dims),
            mesh=mesh,
            in_specs=(P("record", "fibre", None, None), P("record", "fibre", None)) + (P(),) * 7,
            out_specs=(P("record", "fibre", None, None),) + (P(),) * 7,
            check_vma=False,
        )(records, *rest)

    return run
```

```python
import functools

import jax
import jax.numpy as jnp
from jax import lax
from jax.experimental import pallas as pl
from jax.experimental.pallas import tpu as pltpu
from jax.sharding import PartitionSpec as P

F = 64
TAPS = 7
DILATION = 2
HALF = 3
EPS = 1e-05
BF = jnp.bfloat16
F32 = jnp.float32
MESH = pl.DeviceIdType.MESH
NT = (((1,), (1,)), ((), ()))


def mm(a, b):
    return jnp.dot(a, b, preferred_element_type=F32)


def sigmoid(v):
    return 0.5 * jnp.tanh(0.5 * v) + 0.5


def eye():
    return lax.broadcasted_iota(jnp.int32, (F, F), 0) == lax.broadcasted_iota(jnp.int32, (F, F), 1)


def to_col(row):
    return jnp.sum(jnp.where(eye(), jnp.broadcast_to(row, (F, F)), 0.0), axis=1, keepdims=True)


def to_row(col):
    return jnp.sum(jnp.where(eye(), jnp.broadcast_to(col, (F, F)), 0.0), axis=0, keepdims=True)


def wide(row):
    return jnp.broadcast_to(to_col(row), (F, 128))


class Group:
    def __init__(self, n, me, target, send, recv):
        self.n, self.me, self.target, self.send, self.recv = n, me, target, send, recv

    def peers(self):
        return [lax.rem(self.me + d, self.n) for d in range(1, self.n)]

    def copy(self, src, dst, p):
        return pltpu.make_async_remote_copy(
            src_ref=src, dst_ref=dst, send_sem=self.send, recv_sem=self.recv,
            device_id=self.target(p), device_id_type=MESH,
        )

    def spread(self, buf):
        for p in self.peers():
            self.copy(buf.at[self.me], buf.at[self.me], p).start()

    def scatter(self, src, buf):
        for p in self.peers():
            self.copy(src.at[p], buf.at[self.me], p).start()

    def all_bytes(self, buf):
        rest = buf.at[pl.ds(0, self.n - 1)]
        return self.copy(rest, rest, self.me)

    def arrive(self, buf):
        if self.n > 1:
            self.all_bytes(buf).wait_recv()

    def done(self, buf):
        if self.n > 1:
            self.all_bytes(buf).wait_send()


def kernel(
    dims,
    x_ref, lab_ref, wt_ref, bt_ref, wf_ref, gam_ref, bet_ref, wh_ref, bh_ref,
    gr_ref, gwt_ref, gwf_ref, vec_ref,
    wts, wtt, wfb, wfr, xcol, dcol, h1, sl1, z2, sl2, dz2, dz1, par, acc, accr, lab, dl, dll, dlr,
    gt,
    sp1, sz1, sp2, sz2,
    ga, ra, za, fa, gb, rb, zb, fb,
    hs, hr, ds, dr, sem, xs, gs, io,
):
    nf, nx, nz, C, T = dims
    total = float(nf * nx * nz * C * T)
    cells = float(nf * C * T)
    fi = lax.axis_index("fibre")
    ri = lax.axis_index("record")
    xi, zi = ri // nz, lax.rem(ri, nz)

    def plane(i):
        return Group(
            nf * nx, fi * nx + xi, lambda p: (p // nx, lax.rem(p, nx) * nz + zi), sem.at[2 * i], sem.at[2 * i + 1]
        )

    def line(i):
        return Group(nz, zi, lambda p: (fi, xi * nz + p), sem.at[2 * i], sem.at[2 * i + 1])

    def fetch(c):
        return pltpu.make_async_copy(x_ref.at[c], xs.at[c], io.at[c])

    def store(c):
        return pltpu.make_async_copy(gs.at[c], gr_ref.at[c], io.at[C + c])

    for i in range(C):
        fetch(i // 2 if i % 2 == 0 else C - 1 - i // 2).start()

    barrier = pltpu.get_barrier_semaphore()
    for group in (plane(0), line(1)):
        for p in group.peers():
            pl.semaphore_signal(barrier, inc=1, device_id=group.target(p), device_id_type=MESH)

    for k in range(TAPS):
        wts[:, k * F:(k + 1) * F] = wt_ref[k]
    par[0] = wide(bt_ref[...])

    has_l, has_r = fi > 0, fi < nf - 1
    left, right = lax.rem(fi + nf - 1, nf), lax.rem(fi + 1, nf)

    @pl.when(jnp.logical_not(has_l))
    def _():
        for i in range(2 * HALF):
            h1[i] = jnp.zeros((F, T), BF)
        for i in range(HALF):
            dz2[i] = jnp.zeros((F, T), BF)

    @pl.when(jnp.logical_not(has_r))
    def _():
        for i in range(2 * HALF):
            h1[2 * HALF + C + i] = jnp.zeros((F, T), BF)
        for i in range(HALF):
            dz2[HALF + C + i] = jnp.zeros((F, T), BF)

    def halo(c, side):
        slot = c + 2 * HALF + C if side == "l" else c + 2 * HALF - C
        index = c + 2 * HALF if side == "l" else c + 2 * HALF - C
        return pltpu.make_async_remote_copy(
            src_ref=h1.at[c + 2 * HALF],
            dst_ref=h1.at[slot],
            send_sem=hs.at[index],
            recv_sem=hr.at[index],
            device_id=(left if side == "l" else right, ri),
            device_id_type=MESH,
        )

    def halo_arrive(i, side):
        slot = i if side == "l" else i + 2 * HALF + C
        index = i if side == "l" else i + 2 * HALF
        pltpu.make_async_remote_copy(
            src_ref=h1.at[slot], dst_ref=h1.at[slot], send_sem=hs.at[index], recv_sem=hr.at[index],
            device_id=(left if side == "l" else right, ri), device_id_type=MESH,
        ).wait_recv()

    lane = lax.broadcasted_iota(jnp.int32, (F, 128), 1)

    def shifted(src, dst, sign):
        for k in range(TAPS):
            s = sign * DILATION * (k - HALF)
            rows = slice(k * F, (k + 1) * F)
            if s == 0:
                dst[rows, :] = src.astype(BF)
                continue
            r = pltpu.roll(src, (-s) % T, 1)
            dst[rows, :] = r.astype(BF)
            if s > 0:
                dst[rows, T - 128:] = jnp.where(lane < 128 - s, r[:, T - 128:], jnp.zeros((), r.dtype)).astype(BF)
            else:
                dst[rows, :128] = jnp.where(lane >= -s, r[:, :128], jnp.zeros((), r.dtype)).astype(BF)

    def forward(i, carry):
        c = jnp.where(lax.rem(i, 2) == 0, i // 2, C - 1 - i // 2)
        fetch(c).wait()
        shifted(xs[c], xcol.at[c], 1)
        for n in range(0, T, 256):
            pre2 = mm(wts[...], xcol[c, :, n:n + 256])
            for m in range(0, 256, 128):
                cols = slice(n + m, n + m + 128)
                pre = pre2[:, m:m + 128] + par[0]
                s = sigmoid(pre)
                h = pre * s
                h1[c + 2 * HALF, :, cols] = h.astype(BF)
                sl1[c, :, cols] = s + h * (1.0 - s)

        return carry

    def forward_send(i, carry):
        c = jnp.where(lax.rem(i, 2) == 0, i // 2, C - 1 - i // 2)
        forward(i, carry)

        @pl.when(jnp.logical_and(has_l, c < HALF))
        def _():
            halo(c, "l").start()

        @pl.when(jnp.logical_and(has_r, c >= C - HALF))
        def _():
            halo(c, "r").start()

        return carry

    lax.fori_loop(0, 2, forward, 0, unroll=2)
    pl.semaphore_wait(barrier, nf * nx + nz - 2)

    @pl.when(has_l)
    def _():
        halo(0, "l").start()

    @pl.when(has_r)
    def _():
        halo(C - 1, "r").start()

    lax.fori_loop(2, C, forward_send, 0, unroll=6)
    for d in range(HALF):
        @pl.when(has_l)
        def _():
            halo(HALF + d, "l").start()

        @pl.when(has_r)
        def _():
            halo(C - HALF - 1 - d, "r").start()

    for k in range(TAPS):
        wtt[:, k * F:(k + 1) * F] = wt_ref[k].astype(F32).T.astype(BF)
    wfb[...] = jnp.zeros_like(wfb)
    wfr[...] = jnp.zeros_like(wfr)
    for k in range(TAPS):
        w = wf_ref[k]
        wr = wf_ref[TAPS - 1 - k].astype(F32).T.astype(BF)
        for j in range(4):
            wfb[j * F:(j + 1) * F, (j + k) * F:(j + k + 1) * F] = w
            wfr[j * F:(j + 1) * F, (j + k) * F:(j + k + 1) * F] = wr
    for c in range(C):
        lab[c] = lab_ref[c:c + 1, :].astype(F32)
    par[3] = wide(bet_ref[...])
    par[4] = wide(wh_ref[...].astype(F32))
    acc[...] = jnp.zeros_like(acc)
    accr[...] = jnp.zeros_like(accr)

    def fibre_conv(first, count, lo):
        def body(n, carry):
            cols = pl.ds(pl.multiple_of(n * 256, 256), 256)
            data = h1[lo:lo + count + 2 * HALF, :, cols].reshape((count + 2 * HALF) * F, 256)
            out = mm(wfb[:count * F, :(count + 2 * HALF) * F], data)
            z2[first:first + count, :, cols] = out.reshape(count, F, 256)
            return carry

        lax.fori_loop(0, T // 256, body, 0, unroll=4)

    @pl.when(has_l)
    def _():
        for i in range(HALF):
            halo_arrive(HALF + i, "l")

    fibre_conv(HALF, 4, HALF)

    @pl.when(has_r)
    def _():
        for i in range(HALF):
            halo_arrive(i, "r")

    fibre_conv(HALF + 4, 4, HALF + 4)

    def add_up(c, total_):
        for n in range(0, T, 128):
            total_ = total_ + z2[HALF + c, :, n:n + 128]
        return total_

    zero = jnp.zeros((F, 128), F32)
    own_mean = jnp.sum(lax.fori_loop(0, C, add_up, zero, unroll=8), axis=1, keepdims=True) / float(C * T)
    own_wide = jnp.broadcast_to(own_mean, (F, 128))

    def spread_up(c, total_):
        for n in range(0, T, 128):
            d = z2[HALF + c, :, n:n + 128] - own_wide
            total_ = total_ + d * d
        return total_

    own_m2 = jnp.sum(lax.fori_loop(0, C, spread_up, zero, unroll=8), axis=1, keepdims=True)

    def merge(buf, n, count):
        value = buf[...]
        total_ = jnp.sum(value, axis=0)
        d = value - total_[None] * (1.0 / n)
        m2 = jnp.sum(d * d, axis=0) * count
        return jnp.concatenate([total_[:, :F] * (1.0 / n), total_[:, F:] + m2[:, :F]], axis=1)

    def plain(buf):
        return jnp.sum(buf[...], axis=0)

    p1, z1 = plane(0), line(1)
    sp1[p1.me] = jnp.concatenate([to_row(own_mean), to_row(own_m2)], axis=1)
    p1.spread(sp1)

    p1.arrive(sp1)
    sz1[zi] = merge(sp1, nf * nx, float(C * T))
    z1.spread(sz1)

    @pl.when(has_l)
    def _():
        for i in range(HALF):
            halo_arrive(i, "l")
        fibre_conv(0, HALF, 0)

    @pl.when(has_r)
    def _():
        for i in range(HALF):
            halo_arrive(HALF + i, "r")
        fibre_conv(HALF + C, HALF, HALF + C)

    z1.arrive(sz1)
    stats = merge(sz1, nz, float(C * T * nf * nx))
    mean_row = stats[:, :F]
    rstd_row = lax.rsqrt(stats[:, F:] / total + EPS)
    par[1] = wide(mean_row)
    par[2] = wide(gam_ref[...] * rstd_row)

    bias = bh_ref[0, 0]

    def head(c, carry):
        for n in range(0, T, 128):
            cols = slice(n, n + 128)
            zc = z2[HALF + c, :, cols] - par[1]
            act = zc * par[2] + par[3]
            s = sigmoid(act)
            h = act * s
            h2 = h.astype(BF).astype(F32)
            logit = jnp.sum(h2 * par[4], axis=0, keepdims=True) + bias
            target = lab[c, :, cols]
            soft = jnp.maximum(logit, 0.0) + jnp.log1p(jnp.exp(-jnp.abs(logit)))
            accr[0:1, :] += soft - target * logit
            dlogit = sigmoid(logit) - target
            dl[c, :, cols] = dlogit
            dh2 = (dlogit * par[4]).astype(BF).astype(F32)
            dact = dh2 * (s + h * (1.0 - s))
            sl2[HALF + c, :, cols] = dact
            acc[0] += dact
            acc[1] += dact * zc
            acc[2] += dlogit * h2
        return carry

    lax.fori_loop(0, C, head, 0, unroll=4)

    def dl_copy(side):
        i = 0 if side == "l" else 1
        return pltpu.make_async_remote_copy(
            src_ref=dl.at[0:HALF] if side == "l" else dl.at[C - HALF:C], dst_ref=dlr if side == "l" else dll, send_sem=ds.at[i], recv_sem=dr.at[i],
            device_id=(left if side == "l" else right, ri), device_id_type=MESH,
        )

    def dl_arrive(side):
        i = 1 if side == "l" else 0
        buf = dll if side == "l" else dlr
        pltpu.make_async_remote_copy(
            src_ref=buf, dst_ref=buf, send_sem=ds.at[i], recv_sem=dr.at[i],
            device_id=(left if side == "l" else right, ri), device_id_type=MESH,
        ).wait_recv()

    @pl.when(has_l)
    def _():
        dl_copy("l").start()

    @pl.when(has_r)
    def _():
        dl_copy("r").start()

    def lanes(v):
        return jnp.sum(v, axis=1, keepdims=True)

    p2, z2_ = plane(2), line(3)
    sp2[p2.me] = jnp.concatenate([to_row(lanes(acc[0])), to_row(lanes(acc[1]))], axis=1)
    p2.spread(sp2)

    def halo_dact(slot, buf, row):
        for n in range(0, T, 128):
            cols = slice(n, n + 128)
            act = (z2[slot, :, cols] - par[1]) * par[2] + par[3]
            s = sigmoid(act)
            dh2 = (buf[row, :, cols] * par[4]).astype(BF).astype(F32)
            sl2[slot, :, cols] = dh2 * (s + act * s * (1.0 - s))

    def halo_left(i, carry):
        halo_dact(i, dll, i)
        return carry

    def halo_right(i, carry):
        halo_dact(HALF + C + i, dlr, i)
        return carry

    @pl.when(has_l)
    def _():
        dl_arrive("l")
        lax.fori_loop(0, HALF, halo_left, 0)

    p2.arrive(sp2)
    sz2[zi] = plain(sp2)
    z2_.spread(sz2)

    @pl.when(has_r)
    def _():
        dl_arrive("r")
        lax.fori_loop(0, HALF, halo_right, 0)

    z2_.arrive(sz2)
    sums = plain(sz2)
    beta_row = sums[:, :F]
    gamma_row = sums[:, F:] * rstd_row
    vec_ref[2:3, :F] = beta_row / cells
    vec_ref[1:2, :F] = gamma_row / cells
    par[6] = wide(beta_row / total)
    par[7] = wide(gamma_row * rstd_row / total)

    def slope_back(slot, carry):
        for n in range(0, T, 128):
            cols = slice(n, n + 128)
            zc = z2[slot, :, cols] - par[1]
            dz2[slot, :, cols] = (par[2] * (sl2[slot, :, cols] - par[6] - zc * par[7])).astype(BF)
        return carry

    lax.fori_loop(HALF, HALF + C, slope_back, 0, unroll=4)

    @pl.when(has_l)
    def _():
        lax.fori_loop(0, HALF, slope_back, 0)

    @pl.when(has_r)
    def _():
        lax.fori_loop(C + HALF, C + 2 * HALF, slope_back, 0)


    for q in range(2):
        grad = lax.dot_general(
            dz2[HALF + 4 * q:HALF + 4 * q + 4].reshape(4 * F, T),
            h1[HALF + 4 * q:HALF + 4 * q + 10].reshape(10 * F, T),
            NT, preferred_element_type=F32,
        )
        for j in range(4):
            piece = grad[j * F:(j + 1) * F, j * F:(j + TAPS) * F]
            if q == 0 and j == 0:
                gt[:, :TAPS * F] = piece
            else:
                gt[:, :TAPS * F] += piece
    col = lax.broadcasted_iota(jnp.int32, (F, F), 1)

    rows, width = F // nf, 512 // nx

    def pack(src, dst, first, second):
        src[:, TAPS * F:] = jnp.where(col == 0, jnp.broadcast_to(first, (F, F)), jnp.where(col == 1, jnp.broadcast_to(second, (F, F)), 0.0))
        for p in range(nf):
            for q in range(nx):
                dst[p * nx + q] = src[p * rows:(p + 1) * rows, q * width:(q + 1) * width]

    loss_part = jnp.sum(accr[0:1, :], axis=1, keepdims=True)
    pack(gt, ga, lanes(acc[2]), jnp.where(lax.broadcasted_iota(jnp.int32, (F, 1), 0) == 0, jnp.broadcast_to(loss_part, (F, 1)), 0.0))
    a1, a2, a3 = plane(4), line(5), plane(6)
    b1, b2, b3 = plane(7), line(8), plane(9)
    a1.scatter(ga, ra)
    ra[a1.me] = ga[a1.me]

    def fibre_back(q):
        def body(n, carry):
            cols = pl.ds(pl.multiple_of(n * 256, 256), 256)
            data = dz2[4 * q:4 * q + 10, :, cols].reshape(10 * F, 256)
            out = mm(wfr[...], data).reshape(4, F, 256)
            for j in range(4):
                dh = out[j].astype(BF).astype(F32)
                value = (dh * sl1[4 * q + j, :, cols]).astype(BF)
                dz1[4 * q + j, :, cols] = value
                value = value.astype(F32)
                acc[3] += value[:, :128] + value[:, 128:]
            return carry

        lax.fori_loop(0, T // 256, body, 0, unroll=4)

    fibre_back(0)
    fibre_back(1)
    gt[...] = jnp.zeros_like(gt)

    def time_grad(c, carry):
        gt[:, :TAPS * F] += lax.dot_general(dz1[c], xcol[c], NT, preferred_element_type=F32)
        return carry

    lax.fori_loop(0, C, time_grad, 0, unroll=8)
    pack(gt, gb, lanes(acc[3]), jnp.zeros((F, 1), F32))
    b1.scatter(gb, rb)
    rb[b1.me] = gb[b1.me]
    a1.arrive(ra)
    za[zi] = plain(ra)
    a2.spread(za)
    def time_back(c, carry):
        shifted(dz1[c], dcol, -1)
        for n in range(0, T, 256):
            gs[c, :, n:n + 256] = mm(wtt[...], dcol[:, n:n + 256]).astype(BF)
        store(c).start()
        return carry

    lax.fori_loop(0, 4, time_back, 0, unroll=4)
    b1.arrive(rb)
    zb[zi] = plain(rb)
    b2.spread(zb)
    a2.arrive(za)
    fa[a3.me] = plain(za)
    a3.spread(fa)
    lax.fori_loop(4, C, time_back, 0, unroll=4)
    b2.arrive(zb)
    fb[b3.me] = plain(zb)
    b3.spread(fb)

    def unpack(buf, out):
        whole = jnp.concatenate(
            [jnp.concatenate([buf[p * nx + q] for q in range(nx)], axis=1) for p in range(nf)], axis=0
        )
        value = whole * (1.0 / cells)
        for k in range(TAPS):
            out[k] = value[:, k * F:(k + 1) * F]
        return whole[:, TAPS * F:]

    a3.arrive(fa)
    tail = unpack(fa, gwf_ref)
    vec_ref[3:4, :F] = to_row(tail[:, 0:1] / cells)
    vec_ref[4:5, :F] = jnp.broadcast_to(tail[0:1, 1:2] / total, (1, F))
    for c in range(C):
        store(c).wait()
    for group, buf in (
        (p1, sp1), (z1, sz1), (p2, sp2), (z2_, sz2),
        (a1, ga), (a2, za), (a3, fa), (b1, gb), (b2, zb),
    ):
        group.done(buf)

    @pl.when(has_l)
    def _():
        dl_copy("l").wait_send()
        for c in range(2 * HALF):
            halo(c, "l").wait_send()

    @pl.when(has_r)
    def _():
        dl_copy("r").wait_send()
        for c in range(2 * HALF):
            halo(C - 1 - c, "r").wait_send()

    b3.arrive(fb)
    tail = unpack(fb, gwt_ref)
    vec_ref[0:1, :F] = to_row(tail[:, 0:1] / cells)

    b3.done(fb)


def hand_out(
    gr, gwt, gwf, vec, gr_ref, gwt_ref, gbt_ref, gwf_ref, gga_ref, gbe_ref, gwh_ref, loss_ref,
    gr_s, gwt_s, gwf_s, vec_s, gbt_s, gga_s, gbe_s, gwh_s, loss_s, come, go,
):
    half = gr_s.shape[0] // 2
    first, second = pl.ds(0, half), pl.ds(half, half)
    fetch = [
        pltpu.make_async_copy(a, b, come.at[i])
        for i, (a, b) in enumerate((
            (vec, vec_s), (gr.at[first], gr_s.at[first]), (gr.at[second], gr_s.at[second]), (gwt, gwt_s), (gwf, gwf_s),
        ))
    ]
    store = [
        pltpu.make_async_copy(a, b, go.at[i])
        for i, (a, b) in enumerate((
            (gr_s.at[first], gr_ref.at[first]), (gr_s.at[second], gr_ref.at[second]), (gwt_s, gwt_ref), (gwf_s, gwf_ref),
            (gbt_s, gbt_ref), (gga_s, gga_ref), (gbe_s, gbe_ref), (gwh_s, gwh_ref), (loss_s, loss_ref),
        ))
    ]
    for copy in fetch:
        copy.start()
    fetch[0].wait()
    for i, ref in enumerate((gbt_s, gga_s, gbe_s, gwh_s)):
        ref[...] = vec_s[i:i + 1, :F]
    loss_s[...] = vec_s[4:5, 0:1]
    for copy in store[4:]:
        copy.start()
    for a, b in zip(fetch[1:], store[:4]):
        a.wait()
        b.start()
    for copy in store:
        copy.wait()


def local(dims, records, labels, w_time, b_time, w_fibre, gamma, beta, w_head, b_head):
    nf, nx, nz, C, T = dims
    vm = pl.BlockSpec(memory_space=pltpu.VMEM)
    anywhere = pl.BlockSpec(memory_space=pl.ANY)
    S = jax.ShapeDtypeStruct
    V = pltpu.VMEM
    D = pltpu.SemaphoreType.DMA
    n = nf * nx
    rows, width = F // nf, 512 // nx

    def large():
        return [V((n, rows, width), F32), V((n, rows, width), F32), V((nz, rows, width), F32), V((n, rows, width), F32)]

    gr, gwt, gwf, vec = pl.pallas_call(
        functools.partial(kernel, dims),
        out_shape=(S((C, F, T), BF), S((TAPS, F, F), F32), S((TAPS, F, F), F32), S((8, 128), F32)),
        in_specs=[anywhere] + [vm] * 7 + [pl.BlockSpec(memory_space=pltpu.SMEM)],
        out_specs=[anywhere] + [vm] * 3,
        scratch_shapes=[
            V((F, TAPS * F), BF), V((F, TAPS * F), BF), V((4 * F, 10 * F), BF), V((4 * F, 10 * F), BF),
            V((C, TAPS * F, T), BF), V((TAPS * F, T), BF), V((C + 12, F, T), BF), V((C, F, T), F32),
            V((C + 6, F, T), F32), V((C + 6, F, T), F32), V((C + 6, F, T), BF), V((C, F, T), BF),
            V((8, F, 128), F32), V((4, F, 128), F32), V((8, 128), F32),
            V((C, 1, T), F32), V((C, 1, T), F32), V((HALF, 1, T), F32), V((HALF, 1, T), F32),
            V((F, 512), F32),
            V((n, 1, 128), F32), V((nz, 1, 128), F32), V((n, 1, 128), F32), V((nz, 1, 128), F32),
            *large(), *large(),
            D((12,)), D((12,)), D((2,)), D((2,)), D((20,)),
            V((C, F, T), BF), V((C, F, T), BF), D((2 * C,)),
        ],
        compiler_params=pltpu.CompilerParams(
            collective_id=0, has_side_effects=True, vmem_limit_bytes=60 * 1024 * 1024
        ),
    )(
        records[0], labels[0], w_time, b_time.reshape(1, F), w_fibre, gamma.reshape(1, F), beta.reshape(1, F),
        w_head.reshape(1, F), b_head.reshape(1, 1),
    )
    row = S((1, F), F32)
    gr, gwt, gbt, gwf, gga, gbe, gwh, loss = pl.pallas_call(
        hand_out,
        out_shape=(S((C, F, T), BF), S((TAPS, F, F), F32), row, S((TAPS, F, F), F32), row, row, row, S((1, 1), F32)),
        in_specs=[anywhere] * 4,
        out_specs=[anywhere] * 8,
        scratch_shapes=[
            V((C, F, T), BF), V((TAPS, F, F), F32), V((TAPS, F, F), F32), V((8, 128), F32),
            V((1, F), F32), V((1, F), F32), V((1, F), F32), V((1, F), F32), V((1, 1), F32), D((5,)), D((9,)),
        ],
        compiler_params=pltpu.CompilerParams(vmem_limit_bytes=60 * 1024 * 1024),
    )(gr, gwt, gwf, vec)
    return gr[None], gwt, gbt[0], gwf, gga[0], gbe[0], gwh[0], loss[0, 0]


def solution(mesh):
    nf, nr = mesh.shape["fibre"], mesh.shape["record"]
    nx = 4 if nr % 4 == 0 else 1

    def run(records, *rest):
        dims = (nf, nx, nr // nx, records.shape[1] // nf, records.shape[3])
        return jax.shard_map(
            functools.partial(local, dims),
            mesh=mesh,
            in_specs=(P("record", "fibre", None, None), P("record", "fibre", None)) + (P(),) * 7,
            out_specs=(P("record", "fibre", None, None),) + (P(),) * 7,
            check_vma=False,
        )(records, *rest)

    return run
```
